256 devices in a mesh: gx: 8 (over x, z_lo), gy: 32 (over z_hi, y, core).
Axes of the slice: x: 4, y: 4, z: 8 (z_hi: 4, z_lo: 2; z = z_hi * 2 + z_lo), core: 2. Of those that a mesh axis runs over, the one named last changes fastest.
Arguments:
- filtered: float32 [64, 2048, 1024], P(None, 'gy', 'gx'), may hold values from 0 to 1
- upstream: float32 [64, 2048, 1024], P(None, 'gy', 'gx'), may hold values from -24 to 24
- radius_map: int32 [64, 2048, 1024], P(None, 'gy', 'gx'), may hold values from 2 to 12, as said below
- brick_class: int32 [8, 32], P('gx', 'gy'), may hold values from 2 to 12, as said below
- sharpness: float32 [1], replicated, may hold values from 4 to 16
- threshold: float32 [1], replicated, may hold values from 0.35 to 0.65
Outputs:
- sensitivity: float32 [64, 2048, 1024], P(None, 'gy', 'gx')
The draws below stay inside these ranges and needn't reach their ends.
Inputs may be any that keep to these rules, and one draw needn't show every extreme that they name: `radius_map`: each brick holds a cell whose radius equals its brick's brick_class. `brick_class`: some brick has class 12.
All inputs are finite; a program needn't handle non-finite values.
Results may differ from the reference program's by a relative error of at most 0.0001.
Values sent between devices are 32-bit elements; how exact they have to be, the bound alone decides.
No kernel may reach another device: no remote copies, remote signals or barrier semaphores. Data moves between devices by JAX's collectives and lax.ppermute only.
A program may use at most 128 MiB of HBM per device.

```python
import jax
import jax.numpy as jnp
from jax import lax

Z = 64
CX = 128
CY = 64
RMAX = 12
NX = 1024
NY = 2048
BRICKS_X = 8
BRICKS_Y = 32


def brick_levels(key):
    levels = jax.random.randint(jax.random.fold_in(key, 101), (BRICKS_X * BRICKS_Y,), 2, RMAX + 1)
    chosen = jax.random.randint(jax.random.fold_in(key, 102), (), 0, BRICKS_X * BRICKS_Y)
    levels = jnp.where(jnp.arange(BRICKS_X * BRICKS_Y) == chosen, RMAX, levels)
    return levels.reshape(BRICKS_X, BRICKS_Y).astype(jnp.int32)


def draw_brick_class(key, part):
    levels = brick_levels(key)
    return levels


def draw_radius_map(key, part):
    levels = brick_levels(key)
    key = jax.random.fold_in(key, 5)
    ceiling = jnp.repeat(jnp.repeat(levels, CX, axis=0), CY, axis=1).T
    ceiling = jnp.broadcast_to(ceiling[None, :, :], (Z, NY, NX))
    radius = jax.random.randint(key, (Z, NY, NX), 2, RMAX + 1)
    z_index = jax.lax.broadcasted_iota(jnp.int32, (Z, NY, NX), 0)
    y_index = jax.lax.broadcasted_iota(jnp.int32, (Z, NY, NX), 1)
    x_index = jax.lax.broadcasted_iota(jnp.int32, (Z, NY, NX), 2)
    corner = (z_index == 0) & (y_index % CY == 0) & (x_index % CX == 0)
    return jnp.where(corner, ceiling, radius).astype(jnp.int32)


def block_scale(own_key, shape, cuts, smallest, top_value):
    level = 1.0
    for dim, parts in cuts:
        draws = jax.random.uniform(jax.random.fold_in(jax.random.fold_in(own_key, 6), dim), (parts,), jnp.float32, smallest / len(cuts), top_value / len(cuts))
        level = level * jnp.repeat(jnp.exp(draws), shape[dim] // parts).reshape((-1,) + (1,) * (len(shape) - 1 - dim))
    return level


def normal_values(own_key, shape, deviation, most, split=(), kind=jnp.bfloat16):
    values = jax.random.normal(own_key, shape, jnp.float32) * deviation
    if len(split) > 0:
        values = block_scale(own_key, shape, split, -0.22, 0.18) * values
    return jnp.clip(values, min=-most, max=most).astype(kind)


def setup_inputs(seed: int = 0) -> dict:
    key_list = jax.random.split(jax.random.key(seed), 7)
    filtered = jnp.clip(1.0 * jax.random.uniform(key_list[0], (Z, NY, NX), jnp.float32) ** block_scale(key_list[0], (Z, NY, NX), ((1, 32), (2, 8)), -0.2, 0.2), 0.0, 1.0)
    upstream = normal_values(key_list[1], (Z, NY, NX), 4.0, 24.0, ((1, 32), (2, 8)), jnp.float32)
    radius_map = draw_radius_map(jax.random.fold_in(key_list[6], 71), 0)
    brick_class = draw_brick_class(jax.random.fold_in(key_list[6], 71), 0)
    sharpness = jnp.clip(jax.random.uniform(key_list[4], (1,), jnp.float32, 4.0, 16.0), 4.0, 16.0)
    threshold = jnp.clip(jax.random.uniform(key_list[5], (1,), jnp.float32, 0.35, 0.65), 0.35, 0.65)
    return {"filtered": filtered, "upstream": upstream, "radius_map": radius_map, "brick_class": brick_class, "sharpness": sharpness, "threshold": threshold}


def span_sum(radius, position, extent):
    short_low = jnp.maximum(0, radius - 1 - position)
    short_high = jnp.maximum(0, radius - extent + position)
    whole = radius * radius - (short_low * (short_low + 1)) // 2 - (short_high * (short_high + 1)) // 2
    return whole.astype(jnp.float32)


def smear(field, radius, axis):
    margin = RMAX - 1
    kernel = jnp.maximum(0, radius - jnp.abs(jnp.arange(-margin, margin + 1))).astype(jnp.float32)
    moved = jnp.moveaxis(field, axis, -1)
    length = moved.shape[-1]
    flattened = moved.reshape(-1, 1, length)
    result = lax.conv_general_dilated(flattened, kernel.reshape(1, 1, -1), (1,), [(margin, margin)], precision=lax.Precision.HIGHEST)
    return jnp.moveaxis(result.reshape(moved.shape), -1, axis)


def reference(filtered, upstream, radius_map, brick_class, sharpness, threshold):
    ceiling = jnp.repeat(jnp.repeat(brick_class, CX, axis=0), CY, axis=1).T
    reach = jnp.minimum(radius_map, ceiling[None, :, :])
    z_index = lax.broadcasted_iota(jnp.int32, reach.shape, 0)
    y_index = lax.broadcasted_iota(jnp.int32, reach.shape, 1)
    x_index = lax.broadcasted_iota(jnp.int32, reach.shape, 2)
    weight_sum = span_sum(reach, x_index, NX) * span_sum(reach, y_index, NY) * span_sum(reach, z_index, Z)
    steepness = sharpness[0]
    centre = threshold[0]
    tangent = jnp.tanh(steepness * (filtered - centre))
    slope = upstream * steepness * (1.0 - tangent * tangent) / (jnp.tanh(steepness * centre) + jnp.tanh(steepness * (1.0 - centre)))
    source = slope / weight_sum
    total = jnp.zeros(source.shape, jnp.float32)
    for radius in range(2, RMAX + 1):
        masked = jnp.where(reach == radius, source, jnp.zeros_like(source))
        for axis in (2, 1, 0):
            masked = smear(masked, radius, axis)
        total = total + masked
    return total
```

```python
import functools

import jax
import jax.numpy as jnp
import numpy as np
from jax import lax
from jax.experimental import pallas as pl
from jax.experimental.pallas import tpu as pltpu
from jax.sharding import PartitionSpec as P

RMAX = 12
MARGIN = RMAX - 1
CLASS_GROUPS = ((12, 11), (10, 9), (8, 7), (6, 5), (4, 3), (2,))
Z, CY, CX = 64, 64, 128
HALF = CY // 2
ROWS_X = 160
STEPS = 4
VMEM_LIMIT = 60 * 1024 * 1024


def tent(radius, distance):
    return np.maximum(0, radius - np.abs(distance)).astype(np.float32)


def band_tables():
    z = np.arange(Z)
    rows_z = np.zeros((len(CLASS_GROUPS), 2 * Z, 4 * Z), np.float32)
    for group, classes in enumerate(CLASS_GROUPS):
        for place, radius in enumerate(classes):
            band = tent(radius, z[:, None] - z[None, :])
            rows = slice(place * Z, place * Z + Z)
            rows_z[group, rows, 2 * place * Z : (2 * place + 1) * Z] = band
            rows_z[group, rows, (2 * place + 1) * Z : (2 * place + 2) * Z] = band
    source_x = np.arange(CX)
    outside = np.full(5, 4 * CX)
    target_x = np.concatenate(
        [np.arange(CX), np.arange(-MARGIN, 0), outside, np.arange(CX, CX + MARGIN), outside]
    )
    rows_x = np.zeros((RMAX - 1, ROWS_X, 2 * CX), np.float32)
    for radius in range(2, RMAX + 1):
        band = tent(radius, target_x[:, None] - source_x[None, :])
        rows_x[radius - 2] = np.concatenate([band, band], axis=1)
    return rows_z.astype(jnp.bfloat16), rows_x.astype(jnp.bfloat16)


def split(value):
    high = value.astype(jnp.bfloat16)
    low = (value - high.astype(jnp.float32)).astype(jnp.bfloat16)
    return high, low


def span(reach, edge):
    short = jnp.maximum(0.0, reach - edge)
    return reach * reach - 0.5 * (short * short + short)


def smear_kernel(
    place_ref, class_ref, sharp_ref, thresh_ref,
    fil0, fil1, ups0, ups1, rad0, rad1, band_z, band_x,
    main_ref, left_ref, right_ref, up_ref, down_ref,
    high_s, low_s, reach_s, smooth_s, ext_s,
):
    step = pl.program_id(0)
    col, row = place_ref[0], place_ref[1]
    beta, eta = sharp_ref[0], thresh_ref[0]
    one = jnp.ones((8, CX), jnp.float32)
    scale = (beta * one) / (jnp.tanh(beta * eta * one) + jnp.tanh(beta * (1.0 - eta) * one))
    cap = class_ref[0, 0]
    lane = lax.broadcasted_iota(jnp.int32, (8, CX), 1)
    sub = lax.broadcasted_iota(jnp.int32, (8, CX), 0)
    far = jnp.full((8, CX), 4096, jnp.int32)
    edge_x = jnp.minimum(
        jnp.where(col == 0, lane, far), jnp.where(col == pl.num_programs(0) * 2 - 1, CX - 1 - lane, far)
    )
    edge_x = (edge_x + 1).astype(jnp.float32)

    def sources(half, fil, ups, rad):
        def one_row(y, _):
            y_in = (step + half * STEPS) * 8 + y
            edge_y = jnp.minimum(
                jnp.where(row == 0, y_in, 4096), jnp.where(row == 31, CY - 1 - y_in, 4096)
            )
            edge_y = (edge_y + 1).astype(jnp.float32)
            for zt in range(Z // 16):
                parts = []
                for zg in (2 * zt, 2 * zt + 1):
                    at = (pl.ds(zg * 64 + y, 8, stride=8), slice(None))
                    reach = jnp.minimum(rad[at], cap).astype(jnp.float32)
                    bend = jnp.tanh(beta * (fil[at] - eta))
                    slope = ups[at] * scale * (1.0 - bend * bend)
                    weight = span(reach, edge_x) * span(reach, edge_y)
                    if zg in (0, 1, 6, 7):
                        z_in = zg * 8 + sub
                        edge_z = (jnp.minimum(z_in, Z - 1 - z_in) + 1).astype(jnp.float32)
                        weight = weight * span(reach, edge_z)
                    else:
                        weight = weight * (reach * reach)
                    parts.append((slope / weight, reach))
                source = jnp.concatenate([parts[0][0], parts[1][0]], axis=0)
                reach = jnp.concatenate([parts[0][1], parts[1][1]], axis=0)
                high, low = split(source)
                at = (half, y, slice(zt * 16, zt * 16 + 16))
                high_s[at] = high
                low_s[at] = low
                reach_s[at] = reach.astype(jnp.bfloat16)
            return 0

        lax.fori_loop(0, 8, one_row, 0)

    sources(0, fil0, ups0, rad0)
    sources(1, fil1, ups1, rad1)

    def quad(pair, _):
        lines = []
        for j in (2 * pair, 2 * pair + 1):
            wide = lambda ref: jnp.concatenate([ref[0, j], ref[1, j]], axis=1)
            lines.append((wide(high_s), wide(low_s), wide(reach_s)))
        for group, classes in enumerate(CLASS_GROUPS):
            depth = 2 * Z * len(classes)
            held = []
            for high, low, reach in lines:
                pieces = []
                for radius in classes:
                    same = reach == jnp.bfloat16(radius)
                    pieces.append(jnp.where(same, high, jnp.bfloat16(0)))
                    pieces.append(jnp.where(same, low, jnp.bfloat16(0)))
                held.append(
                    jnp.dot(
                        band_z[group, : Z * len(classes), :depth],
                        jnp.concatenate(pieces, axis=0),
                        preferred_element_type=jnp.float32,
                    )
                )
            for place, radius in enumerate(classes):
                stack = []
                for part in held:
                    high, low = split(part[place * Z : place * Z + Z])
                    for side in (slice(0, CX), slice(CX, 2 * CX)):
                        stack.append(jnp.concatenate([high[:, side], low[:, side]], axis=1))
                moved = lax.dot_general(
                    band_x[radius - 2],
                    jnp.concatenate(stack, axis=0),
                    (((1,), (1,)), ((), ())),
                    preferred_element_type=jnp.float32,
                )
                t = step * 8 + pair * 2
                smooth_s[radius - 2, t] = moved[:, :CX]
                smooth_s[radius - 2, t + 1] = moved[:, CX:]
        return 0

    lax.fori_loop(0, 4, quad, 0)

    @pl.when(step == STEPS - 1)
    def _():
        def tile(k, _):
            rows = pl.ds(pl.multiple_of(k * 8, 8), 8)
            total = {}
            for t in range(HALF):
                grown = smooth_s[RMAX - 2, t, rows]
                suffix = grown
                for d in range(MARGIN, -1, -1):
                    if d < MARGIN:
                        if d + 1 >= 2:
                            suffix = suffix + smooth_s[d - 1, t, rows]
                        grown = grown + suffix
                    for target in {t + d, t - d}:
                        total[target] = total[target] + grown if target in total else grown
                ext_s[t - MARGIN + MARGIN, rows] = total.pop(t - MARGIN)
            for target in sorted(total):
                ext_s[target + MARGIN, rows] = total[target]
            return 0

        lax.fori_loop(0, ROWS_X // 8, tile, 0)
        upper = lax.broadcasted_iota(jnp.int32, (ROWS_X, CX), 1) >= Z

        def packed(keep, over):
            first = jnp.concatenate([over[:64], over[128:136], over[144:152]], axis=0)
            second = jnp.concatenate([over[64:128], over[136:144], over[152:160]], axis=0)
            return jnp.where(keep[:80], first, pltpu.roll(second, Z, 1))

        for t in range(HALF):
            full = ext_s[t + MARGIN]
            if t < MARGIN:
                over = ext_s[t + HALF + MARGIN]
                full = full + jnp.where(upper, pltpu.roll(over, Z, 1), 0.0)
                up_ref[t] = packed(upper, over)
            if t >= HALF - MARGIN:
                over = ext_s[t - HALF + MARGIN]
                full = full + jnp.where(upper, 0.0, pltpu.roll(over, Z, 1))
                down_ref[t - (HALF - MARGIN)] = packed(~upper, over)
            main_ref[t] = full[:CX]
            left_ref[t] = full[128:144]
            right_ref[t] = full[144:160]


def smear(place, brick_class, sharpness, threshold, filtered, upstream, radius_map, band_z, band_x):
    smem = pl.BlockSpec(memory_space=pltpu.SMEM)
    flat = [a for a in (filtered, upstream, radius_map)]
    block = [
        pl.BlockSpec((Z, 8, CX), functools.partial(lambda h, i: (0, i + h * STEPS, 0), h)) for h in (0, 1)
    ]
    whole = lambda shape: pl.BlockSpec(shape, lambda i: (0,) * len(shape))
    shapes = [(HALF, CX, CX), (HALF, 16, CX), (HALF, 16, CX), (MARGIN, 80, CX), (MARGIN, 80, CX)]
    return pl.pallas_call(
        smear_kernel_flat,
        grid=(STEPS,),
        out_shape=[jax.ShapeDtypeStruct(s, jnp.float32) for s in shapes],
        in_specs=[smem] * 4
        + [block[0], block[1]] * 3
        + [whole(band_z.shape), whole(band_x.shape)],
        out_specs=[whole(s) for s in shapes],
        scratch_shapes=[
            pltpu.VMEM((2, 8, Z, CX), jnp.bfloat16),
            pltpu.VMEM((2, 8, Z, CX), jnp.bfloat16),
            pltpu.VMEM((2, 8, Z, CX), jnp.bfloat16),
            pltpu.VMEM((RMAX - 1, HALF, ROWS_X, CX), jnp.float32),
            pltpu.VMEM((HALF + 2 * MARGIN, ROWS_X, CX), jnp.float32),
        ],
        compiler_params=pltpu.CompilerParams(vmem_limit_bytes=VMEM_LIMIT),
    )(place, brick_class, sharpness, threshold, *[a for a in flat for _ in (0, 1)], band_z, band_x)


def smear_kernel_flat(*refs):
    refs = list(refs)
    for i in range(4, 10):
        refs[i] = refs[i].reshape(Z * 8, CX)
    smear_kernel(*refs)


def corner_kernel(left, right, from_low, from_high, left_out, right_out):
    upper = lax.broadcasted_iota(jnp.int32, (8, CX), 1) >= Z
    for side, (ref, out) in enumerate(((left, left_out), (right, right_out))):
        rows = slice(64 + 8 * side, 72 + 8 * side)
        for t in range(HALF):
            value = ref[t]
            if t < MARGIN:
                got = from_low[t, rows]
                value = value + jnp.concatenate(
                    [jnp.where(upper, 0.0, pltpu.roll(got, Z, 1)), jnp.where(upper, 0.0, got)], axis=0
                )
            if t >= HALF - MARGIN:
                got = from_high[t - (HALF - MARGIN), rows]
                value = value + jnp.concatenate(
                    [jnp.where(upper, pltpu.roll(got, Z, 1), 0.0), jnp.where(upper, got, 0.0)], axis=0
                )
            out[pl.ds(MARGIN * t, MARGIN)] = value[:MARGIN]


def add_corners(left, right, from_low, from_high):
    return pl.pallas_call(
        corner_kernel,
        out_shape=[jax.ShapeDtypeStruct((HALF * MARGIN, CX), jnp.float32)] * 2,
        compiler_params=pltpu.CompilerParams(vmem_limit_bytes=VMEM_LIMIT),
    )(left, right, from_low, from_high)


def merge_kernel(main, from_low, from_high, from_left, from_right, out, block_s, out_s, sem):
    step = pl.program_id(0)
    upper = lax.broadcasted_iota(jnp.int32, (64, CX), 1) >= Z
    flat = out_s.reshape(Z * CY, CX)

    def copies(i):
        return [
            pltpu.make_async_copy(
                out_s.at[:, pl.ds(h * HALF + i * 8, 8)], out.at[:, pl.ds(h * HALF + i * 8, 8)], sem.at[i, h]
            )
            for h in (0, 1)
        ]

    for i in range(STEPS):

        @pl.when(step == i)
        def _():
            for k in range(8):
                t = i * 8 + k
                value = main[k]
                if t < MARGIN:
                    got = from_low[t, :64]
                    value = value + jnp.concatenate(
                        [jnp.where(upper, 0.0, pltpu.roll(got, Z, 1)), jnp.where(upper, 0.0, got)], axis=0
                    )
                if t >= HALF - MARGIN:
                    got = from_high[t - (HALF - MARGIN), :64]
                    value = value + jnp.concatenate(
                        [jnp.where(upper, pltpu.roll(got, Z, 1), 0.0), jnp.where(upper, got, 0.0)], axis=0
                    )
                block_s[k] = value
                block_s[k, :MARGIN] += from_left[pl.ds(MARGIN * t, MARGIN)]
                block_s[k, CX - MARGIN :] += from_right[pl.ds(MARGIN * t, MARGIN)]
                turned = block_s[k].T
                for h in (0, 1):
                    for zg in range(8):
                        flat[pl.ds(zg * 8 * CY + h * HALF + t, 8, stride=CY), :] = turned[
                            h * Z + zg * 8 : h * Z + zg * 8 + 8
                        ]
            for copy in copies(i):
                copy.start()

    @pl.when(step == STEPS - 1)
    def _():
        for i in range(STEPS):
            for copy in copies(i):
                copy.wait()


def merge(main, from_low, from_high, from_left, from_right):
    whole = lambda shape: pl.BlockSpec(shape, lambda i: (0,) * len(shape))
    halos = (from_low, from_high, from_left, from_right)
    return pl.pallas_call(
        merge_kernel,
        grid=(STEPS,),
        out_shape=jax.ShapeDtypeStruct((Z, CY, CX), jnp.float32),
        in_specs=[pl.BlockSpec((8, CX, CX), lambda i: (i, 0, 0))] + [whole(a.shape) for a in halos],
        out_specs=pl.BlockSpec(memory_space=pl.ANY),
        scratch_shapes=[
            pltpu.VMEM((8, CX, CX), jnp.float32),
            pltpu.VMEM((Z, CY, CX), jnp.float32),
            pltpu.SemaphoreType.DMA((STEPS, 2)),
        ],
        compiler_params=pltpu.CompilerParams(vmem_limit_bytes=VMEM_LIMIT),
    )(main, *halos)


def shifted(value, axis, by):
    length = lax.axis_size(axis)
    return lax.ppermute(value, axis, [(i, i + by) for i in range(length) if 0 <= i + by < length])


def per_device(filtered, upstream, radius_map, brick_class, sharpness, threshold):
    rows_z, rows_x = band_tables()
    place = jnp.stack([lax.axis_index("gx"), lax.axis_index("gy")]).astype(jnp.int32)
    main, left, right, up, down = smear(
        place, brick_class, sharpness, threshold, filtered, upstream, radius_map,
        jnp.asarray(rows_z), jnp.asarray(rows_x),
    )
    from_low = shifted(up, "gy", 1)
    from_high = shifted(down, "gy", -1)
    left, right = add_corners(left, right, from_low, from_high)
    from_left = shifted(right, "gx", 1)
    from_right = shifted(left, "gx", -1)
    return merge(main, from_low, from_high, from_left, from_right)


def solution(mesh):
    return jax.shard_map(
        per_device,
        mesh=mesh,
        in_specs=(
            P(None, "gy", "gx"),
            P(None, "gy", "gx"),
            P(None, "gy", "gx"),
            P("gx", "gy"),
            P(),
            P(),
        ),
        out_specs=P(None, "gy", "gx"),
        check_vma=False,
    )
```

```python
import functools

import jax
import jax.numpy as jnp
import numpy as np
from jax import lax
from jax.experimental import pallas as pl
from jax.experimental.pallas import tpu as pltpu
from jax.sharding import PartitionSpec as P

RMAX = 12
MARGIN = RMAX - 1
Z, CY, CX = 64, 64, 128
HALF = CY // 2
ROWS_X = 160
STEPS = 4
ZROWS = 2
PART = HALF // 2
REACHED = PART + MARGIN
VMEM_LIMIT = 60 * 1024 * 1024


def tent(radius, distance):
    return np.maximum(0, radius - np.abs(distance)).astype(np.float32)


def band_tables():
    z = np.arange(Z)
    outside = np.full(5, 4 * CX)
    source_x = np.arange(CX)
    target_x = np.concatenate(
        [np.arange(CX), np.arange(-MARGIN, 0), outside, np.arange(CX, CX + MARGIN), outside]
    )
    rows_z, rows_x = [], []
    for radius in range(2, RMAX + 1):
        band = np.kron(np.eye(2, dtype=np.float32), tent(radius, z[:, None] - z[None, :]))
        rows_z.append(band)
        rows_x.append(tent(radius, target_x[:, None] - source_x[None, :]))
    return np.stack(rows_z).astype(jnp.bfloat16), np.stack(rows_x).astype(jnp.bfloat16)


def split(value):
    high = value.astype(jnp.bfloat16)
    low = (value - high.astype(jnp.float32)).astype(jnp.bfloat16)
    return high, low


def span(reach, edge):
    short = jnp.maximum(0.0, reach - edge)
    return reach * reach - 0.5 * (short * short + short)


def smear_kernel(part, *refs):
    place_ref, class_ref, sharp_ref, thresh_ref = refs[:4]
    fil, ups, rad = ([ref.reshape(Z * 8, CX) for ref in refs[k : k + 2]] for k in (4, 6, 8))
    band_z, band_x = refs[10:12]
    if part == 0:
        up_ref, down_ref, part_ref = refs[12:15]
    else:
        part_ref, main_ref, left_ref, right_ref = refs[12:16]
    source_s, reach_s, grown_s, smooth_s, ext_s = refs[-5:]
    step = pl.program_id(0)
    col, row = place_ref[0], place_ref[1]
    beta, eta = sharp_ref[0], thresh_ref[0]
    one = jnp.ones((8, CX), jnp.float32)
    scale = (beta * one) / (jnp.tanh(beta * eta * one) + jnp.tanh(beta * (1.0 - eta) * one))
    cap = class_ref[0, 0]
    lane = lax.broadcasted_iota(jnp.int32, (8, CX), 1)
    sub = lax.broadcasted_iota(jnp.int32, (8, CX), 0)
    far = jnp.full((8, CX), 4096, jnp.int32)
    edge_x = jnp.minimum(jnp.where(col == 0, lane, far), jnp.where(col == 7, CX - 1 - lane, far))
    edge_x = (edge_x + 1).astype(jnp.float32)

    def one_row(k, _):
        sides = []
        for half in (0, 1):
            y = k if half == 0 else 7 - k
            from_edge = part * PART + step * 8 + k
            at_edge = row == (0 if half == 0 else 31)
            edge_y = (jnp.where(at_edge, from_edge, 4096) + 1).astype(jnp.float32)
            for zg in range(Z // 8):
                at = (pl.ds(zg * 64 + y, 8, stride=8), slice(None))
                reach = jnp.minimum(rad[half][at], cap).astype(jnp.float32)
                bend = jnp.tanh(beta * (fil[half][at] - eta))
                slope = ups[half][at] * scale * (1.0 - bend * bend)
                weight = span(reach, edge_x) * span(reach, edge_y)
                if zg in (0, 1, 6, 7):
                    z_in = zg * 8 + sub
                    edge_z = (jnp.minimum(z_in, Z - 1 - z_in) + 1).astype(jnp.float32)
                    weight = weight * span(reach, edge_z)
                else:
                    weight = weight * (reach * reach)
                sides.append((slope / weight, reach))
        source = jnp.concatenate([a for a, _ in sides], axis=0).T
        high, low = split(source)
        source_s[k, :, :CX] = high
        source_s[k, :, CX:] = low
        reach_s[k] = jnp.concatenate([b for _, b in sides], axis=0).T.astype(jnp.bfloat16)
        return 0

    lax.fori_loop(0, 8, one_row, 0)

    def along_z(c):
        radius = jnp.bfloat16(c + 2)
        none = jnp.zeros((), jnp.bfloat16)
        both_z = jnp.concatenate([band_z[c], band_z[c]], axis=0)
        for k in range(0, 8, ZROWS):
            pieces = []
            for n in range(k, k + ZROWS):
                same = reach_s[n] == radius
                pieces.append(
                    jnp.concatenate(
                        [jnp.where(same, source_s[n, :, :CX], none), jnp.where(same, source_s[n, :, CX:], none)],
                        axis=1,
                    )
                )
            grown = jnp.dot(jnp.concatenate(pieces, axis=0), both_z, preferred_element_type=jnp.float32)
            high, low = split(grown)
            for n in range(ZROWS):
                rows = slice(n * CX, n * CX + CX)
                line = k + n
                lanes = slice((line % 2) * CX, (line % 2) * CX + CX)
                grown_s[c % 2, line // 2, :CX, lanes] = high[rows]
                grown_s[c % 2, line // 2, CX:, lanes] = low[rows]

    def along_x(c):
        both_x = jnp.concatenate([band_x[c], band_x[c]], axis=1)
        for k in range(4):
            moved = jnp.dot(both_x, grown_s[c % 2, k], preferred_element_type=jnp.float32)
            smooth_s[c, step * 8 + 2 * k] = moved[:, :CX]
            smooth_s[c, step * 8 + 2 * k + 1] = moved[:, CX:]

    along_z(0)
    for c in range(RMAX - 1):
        if c + 1 < RMAX - 1:
            along_z(c + 1)
        along_x(c)

    @pl.when(step == PART // 8 - 1)
    def _():
        first = part * PART - MARGIN

        def keep(t, rows, value):
            if part == 0 and t >= 0:
                part_ref[t, rows] = value
            else:
                ext_s[t - first, rows] = value

        def tile(k, _):
            rows = pl.ds(pl.multiple_of(k * 8, 8), 8)
            total = {}
            if part == 1:
                total = {t: part_ref[t, rows] for t in range(first, REACHED)}
            for t in range(part * PART, part * PART + PART):
                here = t - part * PART
                grown = smooth_s[RMAX - 2, here, rows]
                suffix = grown
                for d in range(MARGIN, -1, -1):
                    if d < MARGIN:
                        if d + 1 >= 2:
                            suffix = suffix + smooth_s[d - 1, here, rows]
                        grown = grown + suffix
                    for target in {t + d, t - d}:
                        total[target] = total[target] + grown if target in total else grown
                keep(t - MARGIN, rows, total.pop(t - MARGIN))
            for target in sorted(total):
                keep(target, rows, total[target])
            return 0

        lax.fori_loop(0, ROWS_X // 8, tile, 0)
        if part == 0:
            upper = lax.broadcasted_iota(jnp.int32, (80, CX), 1) >= Z
            for j in range(MARGIN):
                over = ext_s[j]
                one = jnp.concatenate([over[:64], over[128:136], over[144:152]], axis=0)
                two = jnp.concatenate([over[64:128], over[136:144], over[152:160]], axis=0)
                up_ref[j] = jnp.where(upper, one, pltpu.roll(two, Z, 1))
                down_ref[j] = jnp.where(upper, pltpu.roll(two, Z, 1), one)
        else:
            for t in range(HALF):
                full = part_ref[t] if t < first else ext_s[t - first]
                if t >= HALF - MARGIN:
                    full = full + pltpu.roll(ext_s[2 * HALF - 1 - t - first], Z, 1)
                main_ref[t] = full[:CX]
                left_ref[t] = full[128:144]
                right_ref[t] = full[144:160]


def smear(part, scalars, fields, tables, carried=None):
    block = [
        pl.BlockSpec((Z, 8, CX), lambda i: (0, i + part * 2, 0)),
        pl.BlockSpec((Z, 8, CX), lambda i: (0, 7 - i - part * 2, 0)),
    ]
    whole = lambda shape: pl.BlockSpec(shape, lambda i: (0,) * len(shape))
    partial = (REACHED, ROWS_X, CX)
    if part == 0:
        shapes = [(MARGIN, 80, CX), (MARGIN, 80, CX), partial]
    else:
        shapes = [(HALF, CX, CX), (HALF, 16, CX), (HALF, 16, CX)]
    extra = [] if part == 0 else [carried]
    return pl.pallas_call(
        functools.partial(smear_kernel, part),
        grid=(PART // 8,),
        out_shape=[jax.ShapeDtypeStruct(s, jnp.float32) for s in shapes],
        in_specs=[pl.BlockSpec(memory_space=pltpu.SMEM)] * 4
        + block * 3
        + [whole(a.shape) for a in tables]
        + [whole(a.shape) for a in extra],
        out_specs=[whole(s) for s in shapes],
        scratch_shapes=[
            pltpu.VMEM((8, CX, 2 * CX), jnp.bfloat16),
            pltpu.VMEM((8, CX, CX), jnp.bfloat16),
            pltpu.VMEM((2, 4, 2 * CX, 2 * CX), jnp.bfloat16),
            pltpu.VMEM((RMAX - 1, PART, ROWS_X, CX), jnp.float32),
            pltpu.VMEM((PART + 2 * MARGIN, ROWS_X, CX), jnp.float32),
        ],
        compiler_params=pltpu.CompilerParams(vmem_limit_bytes=VMEM_LIMIT),
        cost_estimate=pl.CostEstimate(flops=8_000_000_000, bytes_accessed=8_000_000, transcendentals=262144),
        name="edge_rows" if part == 0 else "middle_rows",
    )(*scalars, *[a for a in fields for _ in (0, 1)], *tables, *extra)


def arriving(from_low, from_high, rows):
    low, high = from_low[rows], from_high[rows]
    upper = lax.broadcasted_iota(jnp.int32, low.shape, 1) >= Z
    return jnp.concatenate(
        [pltpu.roll(jnp.where(upper, low, high), Z, 1), jnp.where(upper, high, low)], axis=0
    )


def corner_kernel(left, right, from_low, from_high, left_out, right_out):
    for side, (ref, out) in enumerate(((left, left_out), (right, right_out))):
        rows = slice(64 + 8 * side, 72 + 8 * side)
        for t in range(HALF):
            value = ref[t]
            if t < MARGIN:
                j = MARGIN - 1 - t
                value = value + arriving(from_low.at[j], from_high.at[j], rows)
            out[pl.ds(MARGIN * t, MARGIN)] = value[:MARGIN]


def add_corners(left, right, from_low, from_high):
    return pl.pallas_call(
        corner_kernel,
        out_shape=[jax.ShapeDtypeStruct((HALF * MARGIN, CX), jnp.float32)] * 2,
        compiler_params=pltpu.CompilerParams(vmem_limit_bytes=VMEM_LIMIT),
    )(left, right, from_low, from_high)


def merge_kernel(main, from_low, from_high, from_left, from_right, out, block_s, out_s, sem):
    step = pl.program_id(0)
    flat = out_s.reshape(Z * CY, CX)

    def copies(i):
        return [
            pltpu.make_async_copy(
                out_s.at[:, pl.ds(y, 8)], out.at[:, pl.ds(y, 8)], sem.at[i, h]
            )
            for h, y in enumerate((i * 8, CY - 8 - i * 8))
        ]

    for i in range(STEPS):

        @pl.when(step == i)
        def _():
            for k in range(8):
                t = i * 8 + k
                value = main[k]
                if t < MARGIN:
                    j = MARGIN - 1 - t
                    value = value + arriving(from_low.at[j], from_high.at[j], slice(0, 64))
                block_s[k] = value
                block_s[k, :MARGIN] += from_left[pl.ds(MARGIN * t, MARGIN)]
                block_s[k, CX - MARGIN :] += from_right[pl.ds(MARGIN * t, MARGIN)]
                turned = block_s[k].T
                for h, y in enumerate((t, CY - 1 - t)):
                    for zg in range(8):
                        flat[pl.ds(zg * 8 * CY + y, 8, stride=CY), :] = turned[
                            h * Z + zg * 8 : h * Z + zg * 8 + 8
                        ]
            for copy in copies(i):
                copy.start()

    @pl.when(step == STEPS - 1)
    def _():
        for i in range(STEPS):
            for copy in copies(i):
                copy.wait()


def merge(main, from_low, from_high, from_left, from_right):
    whole = lambda shape: pl.BlockSpec(shape, lambda i: (0,) * len(shape))
    halos = (from_low, from_high, from_left, from_right)
    return pl.pallas_call(
        merge_kernel,
        grid=(STEPS,),
        out_shape=jax.ShapeDtypeStruct((Z, CY, CX), jnp.float32),
        in_specs=[pl.BlockSpec((8, CX, CX), lambda i: (i, 0, 0))] + [whole(a.shape) for a in halos],
        out_specs=pl.BlockSpec(memory_space=pl.ANY),
        scratch_shapes=[
            pltpu.VMEM((8, CX, CX), jnp.float32),
            pltpu.VMEM((Z, CY, CX), jnp.float32),
            pltpu.SemaphoreType.DMA((STEPS, 2)),
        ],
        compiler_params=pltpu.CompilerParams(vmem_limit_bytes=VMEM_LIMIT),
    )(main, *halos)


def shifted(value, axis, by):
    length = lax.axis_size(axis)
    return lax.ppermute(value, axis, [(i, i + by) for i in range(length) if 0 <= i + by < length])


def per_device(filtered, upstream, radius_map, brick_class, sharpness, threshold):
    rows_z, rows_x = band_tables()
    place = jnp.stack([lax.axis_index("gx"), lax.axis_index("gy")]).astype(jnp.int32)
    scalars = (place, brick_class, sharpness, threshold)
    fields = (filtered, upstream, radius_map)
    tables = (jnp.asarray(rows_z), jnp.asarray(rows_x))
    up, down, carried = smear(0, scalars, fields, tables)
    from_low = shifted(up, "gy", 1)
    from_high = shifted(down, "gy", -1)
    main, left, right = smear(1, scalars, fields, tables, carried)
    left, right = add_corners(left, right, from_low, from_high)
    from_left = shifted(right, "gx", 1)
    from_right = shifted(left, "gx", -1)
    return merge(main, from_low, from_high, from_left, from_right)


def solution(mesh):
    return jax.shard_map(
        per_device,
        mesh=mesh,
        in_specs=(
            P(None, "gy", "gx"),
            P(None, "gy", "gx"),
            P(None, "gy", "gx"),
            P("gx", "gy"),
            P(),
            P(),
        ),
        out_specs=P(None, "gy", "gx"),
        check_vma=False,
    )
```

```python
import functools

import jax
import jax.numpy as jnp
import numpy as np
from jax import lax
from jax.experimental import pallas as pl
from jax.experimental.pallas import tpu as pltpu
from jax.sharding import PartitionSpec as P

RMAX = 12
MARGIN = RMAX - 1
CLASSES = RMAX - 1
Z, CY, CX = 64, 64, 128
HALF = CY // 2
GROUP = 8
PART = HALF // 2
REACHED = PART + MARGIN
RIM = 16
HALO_ROWS = 480
MIB = 1024 * 1024


def tent(radius, distance):
    return np.maximum(0, radius - np.abs(distance)).astype(np.float32)


def band_tables():
    z, x = np.arange(Z), np.arange(CX)
    outside = np.full(RIM - MARGIN, 8 * CX)
    rim_from = np.concatenate([np.arange(RIM), np.arange(CX - RIM, CX)])
    rim_to = np.concatenate([np.arange(-MARGIN, 0), outside, np.arange(CX, CX + MARGIN), outside])
    rows_z, rows_x, rows_rim = [], [], []
    for radius in range(2, RMAX + 1):
        rows_z.append(np.kron(np.eye(2, dtype=np.float32), tent(radius, z[:, None] - z[None, :])))
        rows_x.append(tent(radius, x[:, None] - x[None, :]))
        rim = tent(radius, rim_to[:, None] - rim_from[None, :])
        rows_rim.append(np.kron(np.eye(4, dtype=np.float32), rim))
    return [jnp.asarray(np.stack(rows).astype(jnp.bfloat16)) for rows in (rows_z, rows_x, rows_rim)]


def split(value):
    high = value.astype(jnp.bfloat16)
    low = (value - high.astype(jnp.float32)).astype(jnp.bfloat16)
    return high, low


def span(reach, edge):
    short = jnp.maximum(0.0, reach - edge)
    return reach * reach - 0.5 * (short * short + short)


def whole(shape):
    return pl.BlockSpec(shape, lambda i: (0,) * len(shape))


def along_z(c, high_low, reach, band_z):
    radius = jnp.bfloat16(c + 2)
    none = jnp.zeros((), jnp.bfloat16)
    pieces = []
    for pair, level in zip(high_low, reach):
        same = level == radius
        pieces.append(jnp.concatenate([jnp.where(same, piece, none) for piece in pair], axis=1))
    both = jnp.concatenate([band_z[c], band_z[c]], axis=0)
    return split(jnp.dot(jnp.concatenate(pieces, axis=0), both, preferred_element_type=jnp.float32))


def spread_y(load, times, total, keep):
    for t in times:
        grown = load(RMAX, t)
        suffix = grown
        for d in range(MARGIN, -1, -1):
            if d < MARGIN:
                if d + 1 >= 2:
                    suffix = suffix + load(d + 1, t)
                grown = grown + suffix
            for target in {t + d, t - d}:
                total[target] = total[target] + grown if target in total else grown
        keep(t - MARGIN, total.pop(t - MARGIN))
    for target in sorted(total):
        keep(target, total[target])


def rim_kernel(
    class_ref, sharp_ref, thresh_ref, fil0, fil1, ups0, ups1, rad0, rad1, band_z, band_rim,
    source_ref, reach_ref, left_ref, right_ref, pair_a, pair_b, level_a, level_b, grown_s, smooth_s, ext_s,
):
    fil, ups, rad = (
        [ref.reshape(Z * GROUP, CX) for ref in pair] for pair in ((fil0, fil1), (ups0, ups1), (rad0, rad1))
    )
    step = pl.program_id(0)
    col, row = lax.axis_index("gx"), lax.axis_index("gy")
    last_col, last_row = lax.axis_size("gx") - 1, lax.axis_size("gy") - 1
    beta, eta = sharp_ref[0], thresh_ref[0]
    one = jnp.ones((8, CX), jnp.float32)
    scale = (beta * one) / (jnp.tanh(beta * eta * one) + jnp.tanh(beta * (1.0 - eta) * one))
    cap = class_ref[0, 0]
    lane = lax.broadcasted_iota(jnp.int32, (8, CX), 1)
    sub = lax.broadcasted_iota(jnp.int32, (8, CX), 0)
    far = jnp.full((8, CX), 4096, jnp.int32)
    edge_x = jnp.minimum(jnp.where(col == 0, lane, far), jnp.where(col == last_col, CX - 1 - lane, far))
    edge_x = (edge_x + 1).astype(jnp.float32)

    def one_row(k, pair_s, level_s):
        sides = []
        for half in (0, 1):
            y = k if half == 0 else GROUP - 1 - k
            at_edge = row == (0 if half == 0 else last_row)
            edge_y = (jnp.where(at_edge, step * GROUP + k, 4096) + 1).astype(jnp.float32)
            for zg in range(Z // 8):
                at = (pl.ds(zg * 8 * GROUP + y, 8, stride=GROUP), slice(None))
                reach = jnp.minimum(rad[half][at], cap).astype(jnp.float32)
                bend = jnp.tanh(beta * (fil[half][at] - eta))
                slope = ups[half][at] * scale * (1.0 - bend * bend)
                weight = span(reach, edge_x) * span(reach, edge_y)
                if zg in (0, 1, 6, 7):
                    z_in = zg * 8 + sub
                    edge_z = (jnp.minimum(z_in, Z - 1 - z_in) + 1).astype(jnp.float32)
                    weight = weight * span(reach, edge_z)
                else:
                    weight = weight * (reach * reach)
                sides.append((slope / weight, reach))
        high, low = split(jnp.concatenate([a for a, _ in sides], axis=0).T)
        level = jnp.concatenate([b for _, b in sides], axis=0).T.astype(jnp.bfloat16)
        source_ref[k, :, :CX] = high
        source_ref[k, :, CX:] = low
        reach_ref[k] = level
        for n, rows in enumerate((slice(0, RIM), slice(CX - RIM, CX))):
            pair_s[k, n, :, :CX] = high[rows]
            pair_s[k, n, :, CX:] = low[rows]
            level_s[k, n] = level[rows]

    def rim_z(c, pair_s, level_s):
        for k in range(0, GROUP, 4):
            both = [(n, side) for n in range(k, k + 4) for side in (0, 1)]
            pairs = [(pair_s[n, side, :, :CX], pair_s[n, side, :, CX:]) for n, side in both]
            high, low = along_z(c, pairs, [level_s[n, side] for n, side in both], band_z)
            lanes = slice(k // 4 * CX, k // 4 * CX + CX)
            grown_s[c % 2, :CX, lanes] = high
            grown_s[c % 2, CX:, lanes] = low

    def rim_x(c):
        both = jnp.concatenate([band_rim[c], band_rim[c]], axis=1)
        moved = jnp.dot(both, grown_s[c % 2], preferred_element_type=jnp.float32)
        for k in range(GROUP):
            lanes = slice(k // 4 * CX, k // 4 * CX + CX)
            rows = slice(k % 4 * 2 * RIM, k % 4 * 2 * RIM + 2 * RIM)
            smooth_s[c, (step - 1) * GROUP + k] = moved[rows, lanes]

    def classes(pair_s, level_s, beside):
        rim_z(0, pair_s, level_s)
        for c in range(CLASSES):
            if c + 1 < CLASSES:
                rim_z(c + 1, pair_s, level_s)
            beside(c)
            rim_x(c)

    def beside(pair_s, level_s):
        def go(c):
            if c < GROUP:
                one_row(c, pair_s, level_s)

        return go

    groups = HALF // GROUP

    @pl.when(step == 0)
    def _():
        @pl.loop(0, GROUP)
        def _(k):
            one_row(k, pair_a, level_a)

    @pl.when((step % 2 == 1) & (step < groups))
    def _():
        classes(pair_a, level_a, beside(pair_b, level_b))

    @pl.when((step % 2 == 0) & (step > 0) & (step < groups))
    def _():
        classes(pair_b, level_b, beside(pair_a, level_a))

    @pl.when(step == groups)
    def _():
        classes(pair_b, level_b, lambda c: None)

        def tile(k, _):
            rows = pl.ds(pl.multiple_of(k * 8, 8), 8)

            def keep(t, value):
                ext_s[t + MARGIN, rows] = value

            spread_y(lambda radius, t: smooth_s[radius - 2, t, rows], range(HALF), {}, keep)
            return 0

        lax.fori_loop(0, 2 * RIM // 8, tile, 0)
        for t in range(-MARGIN, HALF):
            full = ext_s[t + MARGIN]
            if t >= HALF - MARGIN:
                full = full + pltpu.roll(ext_s[2 * HALF - 1 - t + MARGIN], Z, 1)
            left_ref[pl.ds(MARGIN * (t + MARGIN), MARGIN)] = full[:MARGIN]
            right_ref[pl.ds(MARGIN * (t + MARGIN), MARGIN)] = full[RIM : RIM + MARGIN]
        for ref in (left_ref, right_ref):
            spare = HALO_ROWS - MARGIN * (HALF + MARGIN)
            ref[pl.ds(HALO_ROWS - spare, spare)] = jnp.zeros((spare, CX), jnp.float32)


def rim(scalars, fields, band_z, band_rim):
    groups = HALF // GROUP
    now = lambda i: jnp.minimum(i, groups - 1)
    block = [
        pl.BlockSpec((Z, GROUP, CX), lambda i: (0, now(i), 0)),
        pl.BlockSpec((Z, GROUP, CX), lambda i: (0, 2 * groups - 1 - now(i), 0)),
    ]
    halo = (HALO_ROWS, CX)
    return pl.pallas_call(
        rim_kernel,
        grid=(groups + 1,),
        out_shape=[
            jax.ShapeDtypeStruct((HALF, CX, 2 * CX), jnp.bfloat16),
            jax.ShapeDtypeStruct((HALF, CX, CX), jnp.bfloat16),
            jax.ShapeDtypeStruct(halo, jnp.float32),
            jax.ShapeDtypeStruct(halo, jnp.float32),
        ],
        in_specs=[pl.BlockSpec(memory_space=pltpu.SMEM)] * 3
        + block * 3
        + [whole(band_z.shape), whole(band_rim.shape)],
        out_specs=[
            pl.BlockSpec((GROUP, CX, 2 * CX), lambda i: (now(i), 0, 0)),
            pl.BlockSpec((GROUP, CX, CX), lambda i: (now(i), 0, 0)),
            whole(halo),
            whole(halo),
        ],
        scratch_shapes=[
            pltpu.VMEM((GROUP, 2, RIM, 2 * CX), jnp.bfloat16),
            pltpu.VMEM((GROUP, 2, RIM, 2 * CX), jnp.bfloat16),
            pltpu.VMEM((GROUP, 2, RIM, CX), jnp.bfloat16),
            pltpu.VMEM((GROUP, 2, RIM, CX), jnp.bfloat16),
            pltpu.VMEM((2, 2 * CX, 2 * CX), jnp.bfloat16),
            pltpu.VMEM((CLASSES, HALF, 2 * RIM, CX), jnp.float32),
            pltpu.VMEM((HALF + 2 * MARGIN, 2 * RIM, CX), jnp.float32),
        ],
        compiler_params=pltpu.CompilerParams(vmem_limit_bytes=60 * MIB),
        cost_estimate=pl.CostEstimate(flops=4_000_000_000, bytes_accessed=11_000_000, transcendentals=524288),
        name="source_and_rim",
    )(*scalars, *[a for a in fields for _ in (0, 1)], band_z, band_rim)


def rows_kernel(part, *refs):
    source_ref, reach_ref, band_z, band_x = refs[:4]
    if part == 0:
        halo_ref, part_ref = refs[4:6]
        grown_s, smooth_s = refs[6:]
    else:
        part_ref, from_left, from_right, edge_ref, out_ref = refs[4:9]
        grown_s, smooth_s, ext_s, out_s, sem = refs[9:]
    step = pl.program_id(0)

    def main_z(c):
        for k in range(0, GROUP, 2):
            pairs = [(source_ref[n, :, :CX], source_ref[n, :, CX:]) for n in (k, k + 1)]
            high, low = along_z(c, pairs, [reach_ref[n] for n in (k, k + 1)], band_z)
            for n in (0, 1):
                here = slice(n * CX, n * CX + CX)
                grown_s[c % 2, k // 2, :CX, here] = high[here]
                grown_s[c % 2, k // 2, CX:, here] = low[here]

    def main_x(c):
        both = jnp.concatenate([band_x[c], band_x[c]], axis=1)
        for k in range(GROUP // 2):
            moved = jnp.dot(both, grown_s[c % 2, k], preferred_element_type=jnp.float32)
            smooth_s[c, step * GROUP + 2 * k] = moved[:, :CX]
            smooth_s[c, step * GROUP + 2 * k + 1] = moved[:, CX:]

    main_z(0)
    for c in range(CLASSES):
        if c + 1 < CLASSES:
            main_z(c + 1)
        main_x(c)

    @pl.when(step == PART // GROUP - 1)
    def _():
        start = part * PART

        def tile(k, _):
            rows = pl.ds(pl.multiple_of(k * 8, 8), 8)

            def keep(t, value):
                if part == 1:
                    ext_s[t, rows] = value
                elif t < 0:
                    halo_ref[t + MARGIN, rows] = value
                else:
                    part_ref[t, rows] = value

            total = {t: part_ref[t, rows] for t in range(start - MARGIN, REACHED)} if part == 1 else {}
            load = lambda radius, t: smooth_s[radius - 2, t - start, rows]
            spread_y(load, range(start, start + PART), total, keep)
            return 0

        lax.fori_loop(0, CX // 8, tile, 0)
        if part == 1:
            flat = out_s.reshape(Z * PART * 2, CX)
            for t in range(HALF):
                at = edge_ref.at[t] if t < PART else ext_s.at[t]
                if t < PART:
                    at[...] = part_ref[t] if t < start - MARGIN else ext_s[t]
                elif t >= HALF - MARGIN:
                    at[...] += pltpu.roll(ext_s[2 * HALF - 1 - t], Z, 1)
                halo = pl.ds(MARGIN * (t + MARGIN), MARGIN)
                at[:MARGIN] += from_left[halo]
                at[CX - MARGIN :] += from_right[halo]
                if t >= PART:
                    turned = at[...].T
                    for h, y in enumerate((t - PART, HALF + PART - 1 - t)):
                        for zg in range(Z // 8):
                            rows = slice(h * Z + zg * 8, h * Z + zg * 8 + 8)
                            flat[pl.ds(zg * 8 * HALF + y, 8, stride=HALF), :] = turned[rows]
            copy = pltpu.make_async_copy(out_s, out_ref.at[:, pl.ds(PART, HALF)], sem)
            copy.start()
            copy.wait()


def spread_rows(part, source, reach, band_z, band_x, *extra):
    partial = (REACHED, CX, CX)
    scratch = [
        pltpu.VMEM((2, GROUP // 2, 2 * CX, 2 * CX), jnp.bfloat16),
        pltpu.VMEM((CLASSES, PART, CX, CX), jnp.float32),
    ]
    if part == 0:
        shapes = [(MARGIN, CX, CX), partial]
        out_specs = [whole(s) for s in shapes]
    else:
        shapes = [(PART, CX, CX), (Z, CY, CX)]
        out_specs = [whole(shapes[0]), pl.BlockSpec(memory_space=pl.ANY)]
        scratch += [
            pltpu.VMEM((HALF + MARGIN, CX, CX), jnp.float32),
            pltpu.VMEM((Z, HALF, CX), jnp.float32),
            pltpu.SemaphoreType.DMA(()),
        ]
    steps = PART // GROUP
    return pl.pallas_call(
        functools.partial(rows_kernel, part),
        grid=(steps,),
        out_shape=[jax.ShapeDtypeStruct(s, jnp.float32) for s in shapes],
        in_specs=[
            pl.BlockSpec((GROUP, CX, 2 * CX), lambda i: (i + part * steps, 0, 0)),
            pl.BlockSpec((GROUP, CX, CX), lambda i: (i + part * steps, 0, 0)),
            whole(band_z.shape),
            whole(band_x.shape),
        ]
        + [whole(a.shape) for a in extra],
        out_specs=out_specs,
        scratch_shapes=scratch,
        compiler_params=pltpu.CompilerParams(vmem_limit_bytes=40 * MIB),
        cost_estimate=pl.CostEstimate(flops=8_000_000_000, bytes_accessed=8_000_000, transcendentals=0),
        name="edge_rows" if part == 0 else "middle_rows",
    )(source, reach, band_z, band_x, *extra)


def pack_kernel(halo, from_left, from_right, up_ref, down_ref, line_s):
    upper = lax.broadcasted_iota(jnp.int32, (64, CX), 1) >= Z
    for j in range(MARGIN):
        rows = pl.ds(MARGIN * j, MARGIN)
        line_s[...] = halo[j]
        line_s[:MARGIN] += from_left[rows]
        line_s[CX - MARGIN :] += from_right[rows]
        one, two = line_s[:64], pltpu.roll(line_s[64:], Z, 1)
        up_ref[j] = jnp.where(upper, one, two)
        down_ref[j] = jnp.where(upper, two, one)


def pack(halo, from_left, from_right):
    return pl.pallas_call(
        pack_kernel,
        out_shape=[jax.ShapeDtypeStruct((MARGIN, 64, CX), jnp.float32)] * 2,
        scratch_shapes=[pltpu.VMEM((CX, CX), jnp.float32)],
        compiler_params=pltpu.CompilerParams(vmem_limit_bytes=8 * MIB),
        name="pack_halo",
    )(halo, from_left, from_right)


def merge_kernel(edge, from_low, from_high, _, out, out_s, sem):
    step = pl.program_id(0)
    upper = lax.broadcasted_iota(jnp.int32, (64, CX), 1) >= Z

    def copies(i):
        return [
            pltpu.make_async_copy(out_s.at[i, h], out.at[:, pl.ds(y, GROUP)], sem.at[i, h])
            for h, y in enumerate((i * GROUP, CY - GROUP - i * GROUP))
        ]

    for i in range(PART // GROUP):

        @pl.when(step == i)
        def _():
            for k in range(GROUP):
                value = edge[k]
                if i * GROUP + k < MARGIN:
                    j = MARGIN - 1 - i * GROUP - k
                    low, high = from_low[j], from_high[j]
                    value = value + jnp.concatenate(
                        [pltpu.roll(jnp.where(upper, low, high), Z, 1), jnp.where(upper, high, low)], axis=0
                    )
                turned = value.T
                for h, y in enumerate((k, GROUP - 1 - k)):
                    flat = out_s.at[i, h].reshape(Z * GROUP, CX)
                    for zg in range(Z // 8):
                        rows = slice(h * Z + zg * 8, h * Z + zg * 8 + 8)
                        flat[pl.ds(zg * 8 * GROUP + y, 8, stride=GROUP), :] = turned[rows]
            for copy in copies(i):
                copy.start()

    @pl.when(step == PART // GROUP - 1)
    def _():
        for i in range(PART // GROUP):
            for copy in copies(i):
                copy.wait()


def merge(edge, from_low, from_high, out):
    return pl.pallas_call(
        merge_kernel,
        grid=(PART // GROUP,),
        out_shape=jax.ShapeDtypeStruct((Z, CY, CX), jnp.float32),
        in_specs=[
            pl.BlockSpec((GROUP, CX, CX), lambda i: (i, 0, 0)),
            whole(from_low.shape),
            whole(from_high.shape),
            pl.BlockSpec(memory_space=pl.ANY),
        ],
        out_specs=pl.BlockSpec(memory_space=pl.ANY),
        scratch_shapes=[
            pltpu.VMEM((PART // GROUP, 2, Z, GROUP, CX), jnp.float32),
            pltpu.SemaphoreType.DMA((PART // GROUP, 2)),
        ],
        input_output_aliases={3: 0},
        compiler_params=pltpu.CompilerParams(vmem_limit_bytes=8 * MIB),
        name="merge_rows",
    )(edge, from_low, from_high, out)


def shifted(value, axis, by):
    length = lax.axis_size(axis)
    return lax.ppermute(value, axis, [(i, i + by) for i in range(length) if 0 <= i + by < length])


def per_device(filtered, upstream, radius_map, brick_class, sharpness, threshold):
    band_z, band_x, band_rim = band_tables()
    source, reach, left, right = rim(
        (brick_class, sharpness, threshold), (filtered, upstream, radius_map), band_z, band_rim
    )
    from_left = shifted(right, "gx", 1)
    from_right = shifted(left, "gx", -1)
    halo, partial = spread_rows(0, source, reach, band_z, band_x)
    up, down = pack(halo, from_left, from_right)
    from_low = shifted(up, "gy", 1)
    from_high = shifted(down, "gy", -1)
    edge, out = spread_rows(1, source, reach, band_z, band_x, partial, from_left, from_right)
    return merge(edge, from_low, from_high, out)


def solution(mesh):
    return jax.shard_map(
        per_device,
        mesh=mesh,
        in_specs=(
            P(None, "gy", "gx"),
            P(None, "gy", "gx"),
            P(None, "gy", "gx"),
            P("gx", "gy"),
            P(),
            P(),
        ),
        out_specs=P(None, "gy", "gx"),
        check_vma=False,
    )
```

```python
import functools

import jax
import jax.numpy as jnp
import numpy as np
from jax import lax
from jax.experimental import pallas as pl
from jax.experimental.pallas import tpu as pltpu
from jax.sharding import PartitionSpec as P

RMAX = 12
MARGIN = RMAX - 1
CLASSES = RMAX - 1
Z, CY, CX = 64, 64, 128
HALF = CY // 2
GROUP = 8
PART = HALF // 2
REACHED = PART + MARGIN
RIM = 16
RIM_AHEAD = 4
MAIN_AHEAD = 2
MAIN_SLOTS = 4
HALO_ROWS = 480
MIB = 1024 * 1024


def tent(radius, distance):
    return np.maximum(0, radius - np.abs(distance)).astype(np.float32)


def band_tables():
    z, x = np.arange(Z), np.arange(CX)
    outside = np.full(RIM - MARGIN, 8 * CX)
    rim_from = np.concatenate([np.arange(RIM), np.arange(CX - RIM, CX)])
    rim_to = np.concatenate([np.arange(-MARGIN, 0), outside, np.arange(CX, CX + MARGIN), outside])
    rows_z, rows_x, rows_rim = [], [], []
    for radius in range(2, RMAX + 1):
        rows_z.append(np.kron(np.eye(2, dtype=np.float32), tent(radius, z[:, None] - z[None, :])))
        rows_x.append(tent(radius, x[:, None] - x[None, :]))
        rim = tent(radius, rim_to[:, None] - rim_from[None, :])
        rows_rim.append(np.kron(np.eye(4, dtype=np.float32), rim))
    return [jnp.asarray(np.stack(rows).astype(jnp.bfloat16)) for rows in (rows_z, rows_x, rows_rim)]


def split(value):
    high = value.astype(jnp.bfloat16)
    low = (value - high.astype(jnp.float32)).astype(jnp.bfloat16)
    return high, low


def span(reach, edge):
    short = jnp.maximum(0.0, reach - edge)
    return reach * reach - 0.5 * (short * short + short)


def whole(shape):
    return pl.BlockSpec(shape, lambda i: (0,) * len(shape))


def along_z(c, high_low, reach, band_z):
    radius = jnp.bfloat16(c + 2)
    none = jnp.zeros((), jnp.bfloat16)
    pieces = []
    for pair, level in zip(high_low, reach):
        same = level == radius
        pieces.append(jnp.concatenate([jnp.where(same, piece, none) for piece in pair], axis=1))
    both = jnp.concatenate([band_z[c], band_z[c]], axis=0)
    return split(jnp.dot(jnp.concatenate(pieces, axis=0), both, preferred_element_type=jnp.float32))


def spread_y(load, times, total, keep):
    for t in times:
        grown = load(RMAX, t)
        suffix = grown
        for d in range(MARGIN, -1, -1):
            if d < MARGIN:
                if d + 1 >= 2:
                    suffix = suffix + load(d + 1, t)
                grown = grown + suffix
            for target in {t + d, t - d}:
                total[target] = total[target] + grown if target in total else grown
        keep(t - MARGIN, total.pop(t - MARGIN))
    for target in sorted(total):
        keep(target, total[target])


def rim_kernel(
    class_ref, sharp_ref, thresh_ref, fil0, fil1, ups0, ups1, rad0, rad1, band_z, band_rim,
    source_ref, reach_ref, left_ref, right_ref, pair_a, pair_b, level_a, level_b, grown_s, smooth_s, ext_s,
):
    fil, ups, rad = (
        [ref.reshape(Z * GROUP, CX) for ref in pair] for pair in ((fil0, fil1), (ups0, ups1), (rad0, rad1))
    )
    step = pl.program_id(0)
    col, row = lax.axis_index("gx"), lax.axis_index("gy")
    last_col, last_row = lax.axis_size("gx") - 1, lax.axis_size("gy") - 1
    beta, eta = sharp_ref[0], thresh_ref[0]
    one = jnp.ones((8, CX), jnp.float32)
    scale = (beta * one) / (jnp.tanh(beta * eta * one) + jnp.tanh(beta * (1.0 - eta) * one))
    cap = class_ref[0, 0]
    lane = lax.broadcasted_iota(jnp.int32, (8, CX), 1)
    sub = lax.broadcasted_iota(jnp.int32, (8, CX), 0)
    far = jnp.full((8, CX), 4096, jnp.int32)
    edge_x = jnp.minimum(jnp.where(col == 0, lane, far), jnp.where(col == last_col, CX - 1 - lane, far))
    edge_x = (edge_x + 1).astype(jnp.float32)

    def one_row(k, pair_s, level_s):
        sides = []
        for half in (0, 1):
            y = k if half == 0 else GROUP - 1 - k
            at_edge = row == (0 if half == 0 else last_row)
            edge_y = (jnp.where(at_edge, step * GROUP + k, 4096) + 1).astype(jnp.float32)
            for zg in range(Z // 8):
                at = (pl.ds(zg * 8 * GROUP + y, 8, stride=GROUP), slice(None))
                reach = jnp.minimum(rad[half][at], cap).astype(jnp.float32)
                bend = jnp.tanh(beta * (fil[half][at] - eta))
                slope = ups[half][at] * scale * (1.0 - bend * bend)
                weight = span(reach, edge_x) * span(reach, edge_y)
                if zg in (0, 1, 6, 7):
                    z_in = zg * 8 + sub
                    edge_z = (jnp.minimum(z_in, Z - 1 - z_in) + 1).astype(jnp.float32)
                    weight = weight * span(reach, edge_z)
                else:
                    weight = weight * (reach * reach)
                sides.append((slope / weight, reach))
        high, low = split(jnp.concatenate([a for a, _ in sides], axis=0).T)
        level = jnp.concatenate([b for _, b in sides], axis=0).T.astype(jnp.bfloat16)
        source_ref[k, :, :CX] = high
        source_ref[k, :, CX:] = low
        reach_ref[k] = level
        for n, rows in enumerate((slice(0, RIM), slice(CX - RIM, CX))):
            pair_s[k, n, :, :CX] = high[rows]
            pair_s[k, n, :, CX:] = low[rows]
            level_s[k, n] = level[rows]

    def rim_z(c, pair_s, level_s):
        for k in range(0, GROUP, 4):
            both = [(n, side) for n in range(k, k + 4) for side in (0, 1)]
            pairs = [(pair_s[n, side, :, :CX], pair_s[n, side, :, CX:]) for n, side in both]
            high, low = along_z(c, pairs, [level_s[n, side] for n, side in both], band_z)
            lanes = slice(k // 4 * CX, k // 4 * CX + CX)
            grown_s[c, :CX, lanes] = high
            grown_s[c, CX:, lanes] = low

    def rim_x(c):
        both = jnp.concatenate([band_rim[c], band_rim[c]], axis=1)
        moved = jnp.dot(both, grown_s[c], preferred_element_type=jnp.float32)
        for k in range(GROUP):
            lanes = slice(k // 4 * CX, k // 4 * CX + CX)
            rows = slice(k % 4 * 2 * RIM, k % 4 * 2 * RIM + 2 * RIM)
            smooth_s[c, (step - 1) * GROUP + k] = moved[rows, lanes]

    def classes(pair_s, level_s, beside):
        for c in range(RIM_AHEAD):
            rim_z(c, pair_s, level_s)
        for c in range(CLASSES):
            if c + RIM_AHEAD < CLASSES:
                rim_z(c + RIM_AHEAD, pair_s, level_s)
            beside(c)
            rim_x(c)

    def beside(pair_s, level_s):
        def go(c):
            if c < GROUP:
                one_row(c, pair_s, level_s)

        return go

    groups = HALF // GROUP

    @pl.when(step == 0)
    def _():
        @pl.loop(0, GROUP)
        def _(k):
            one_row(k, pair_a, level_a)

    @pl.when((step % 2 == 1) & (step < groups))
    def _():
        classes(pair_a, level_a, beside(pair_b, level_b))

    @pl.when((step % 2 == 0) & (step > 0) & (step < groups))
    def _():
        classes(pair_b, level_b, beside(pair_a, level_a))

    @pl.when(step == groups)
    def _():
        classes(pair_b, level_b, lambda c: None)

        def tile(k, _):
            rows = pl.ds(pl.multiple_of(k * 8, 8), 8)

            def keep(t, value):
                ext_s[t + MARGIN, rows] = value

            spread_y(lambda radius, t: smooth_s[radius - 2, t, rows], range(HALF), {}, keep)
            return 0

        lax.fori_loop(0, 2 * RIM // 8, tile, 0)
        for t in range(-MARGIN, HALF):
            full = ext_s[t + MARGIN]
            if t >= HALF - MARGIN:
                full = full + pltpu.roll(ext_s[2 * HALF - 1 - t + MARGIN], Z, 1)
            left_ref[pl.ds(MARGIN * (t + MARGIN), MARGIN)] = full[:MARGIN]
            right_ref[pl.ds(MARGIN * (t + MARGIN), MARGIN)] = full[RIM : RIM + MARGIN]
        for ref in (left_ref, right_ref):
            spare = HALO_ROWS - MARGIN * (HALF + MARGIN)
            ref[pl.ds(HALO_ROWS - spare, spare)] = jnp.zeros((spare, CX), jnp.float32)


def rim(scalars, fields, band_z, band_rim):
    groups = HALF // GROUP
    now = lambda i: jnp.minimum(i, groups - 1)
    block = [
        pl.BlockSpec((Z, GROUP, CX), lambda i: (0, now(i), 0)),
        pl.BlockSpec((Z, GROUP, CX), lambda i: (0, 2 * groups - 1 - now(i), 0)),
    ]
    halo = (HALO_ROWS, CX)
    return pl.pallas_call(
        rim_kernel,
        grid=(groups + 1,),
        out_shape=[
            jax.ShapeDtypeStruct((HALF, CX, 2 * CX), jnp.bfloat16),
            jax.ShapeDtypeStruct((HALF, CX, CX), jnp.bfloat16),
            jax.ShapeDtypeStruct(halo, jnp.float32),
            jax.ShapeDtypeStruct(halo, jnp.float32),
        ],
        in_specs=[pl.BlockSpec(memory_space=pltpu.SMEM)] * 3
        + block * 3
        + [whole(band_z.shape), whole(band_rim.shape)],
        out_specs=[
            pl.BlockSpec((GROUP, CX, 2 * CX), lambda i: (now(i), 0, 0)),
            pl.BlockSpec((GROUP, CX, CX), lambda i: (now(i), 0, 0)),
            whole(halo),
            whole(halo),
        ],
        scratch_shapes=[
            pltpu.VMEM((GROUP, 2, RIM, 2 * CX), jnp.bfloat16),
            pltpu.VMEM((GROUP, 2, RIM, 2 * CX), jnp.bfloat16),
            pltpu.VMEM((GROUP, 2, RIM, CX), jnp.bfloat16),
            pltpu.VMEM((GROUP, 2, RIM, CX), jnp.bfloat16),
            pltpu.VMEM((CLASSES, 2 * CX, 2 * CX), jnp.bfloat16),
            pltpu.VMEM((CLASSES, HALF, 2 * RIM, CX), jnp.float32),
            pltpu.VMEM((HALF + 2 * MARGIN, 2 * RIM, CX), jnp.float32),
        ],
        compiler_params=pltpu.CompilerParams(vmem_limit_bytes=24 * MIB),
        cost_estimate=pl.CostEstimate(flops=4_000_000_000, bytes_accessed=11_000_000, transcendentals=524288),
        name="source_and_rim",
    )(*scalars, *[a for a in fields for _ in (0, 1)], band_z, band_rim)


def rows_kernel(part, *refs):
    source_ref, reach_ref, band_z, band_x = refs[:4]
    if part == 0:
        halo_ref, part_ref = refs[4:6]
        grown_s, smooth_s = refs[6:]
    else:
        part_ref, from_left, from_right, edge_ref, out_ref = refs[4:9]
        grown_s, smooth_s, ext_s, out_s, sem = refs[9:]
    step = pl.program_id(0)
    start = part * PART

    def main_z(c):
        for k in range(0, GROUP, 2):
            pairs = [(source_ref[n, :, :CX], source_ref[n, :, CX:]) for n in (k, k + 1)]
            high, low = along_z(c, pairs, [reach_ref[n] for n in (k, k + 1)], band_z)
            for n in (0, 1):
                here = slice(n * CX, n * CX + CX)
                grown_s[c % MAIN_SLOTS, k // 2, :CX, here] = high[here]
                grown_s[c % MAIN_SLOTS, k // 2, CX:, here] = low[here]

    def main_x(c, group):
        both = jnp.concatenate([band_x[c], band_x[c]], axis=1)
        for k in range(GROUP // 2):
            moved = jnp.dot(both, grown_s[c % MAIN_SLOTS, k], preferred_element_type=jnp.float32)
            smooth_s[c, group * GROUP + 2 * k] = moved[:, :CX]
            smooth_s[c, group * GROUP + 2 * k + 1] = moved[:, CX:]

    def classes(group, beside):
        for c in range(MAIN_AHEAD):
            main_z(c)
        for c in range(CLASSES):
            if c + MAIN_AHEAD < CLASSES:
                main_z(c + MAIN_AHEAD)
            beside(c)
            main_x(c, group)

    def tile(group, rows):
        first = start + group * GROUP

        def place(t):
            if part == 1:
                return ext_s, t
            return (halo_ref, t + MARGIN) if t < 0 else (part_ref, t)

        def keep(t, value):
            ref, at = place(t)
            ref[at, rows] = value

        total = {}
        for t in range(first - MARGIN, first + MARGIN):
            if group > 0:
                ref, at = place(t)
                total[t] = ref[at, rows]
            elif part == 1 and t < REACHED:
                total[t] = part_ref[t, rows]
        load = lambda radius, t: smooth_s[radius - 2, t - start, rows]
        spread_y(load, range(first, first + GROUP), total, keep)

    tiles = CX // 8

    def tiles_beside(c):
        for k in range(c * tiles // CLASSES, (c + 1) * tiles // CLASSES):
            tile(0, slice(k * 8, k * 8 + 8))

    @pl.when(step == 0)
    def _():
        classes(0, lambda c: None)

    @pl.when(step == 1)
    def _():
        classes(1, tiles_beside)

        @pl.loop(0, tiles)
        def _(k):
            tile(1, pl.ds(pl.multiple_of(k * 8, 8), 8))

        if part == 1:
            flat = out_s.reshape(Z * HALF, CX)
            copies = [
                pltpu.make_async_copy(
                    out_s.at[:, pl.ds(y, GROUP)], out_ref.at[:, pl.ds(PART + y, GROUP)], sem.at[n]
                )
                for n, y in enumerate((0, HALF - GROUP, GROUP, HALF - 2 * GROUP))
            ]
            for t in [*range(PART, HALF), *range(PART)]:
                at = edge_ref.at[t] if t < PART else ext_s.at[t]
                if t < PART:
                    at[...] = part_ref[t] if t < start - MARGIN else ext_s[t]
                elif t >= HALF - MARGIN:
                    at[...] += pltpu.roll(ext_s[2 * HALF - 1 - t], Z, 1)
                halo = pl.ds(MARGIN * (t + MARGIN), MARGIN)
                at[:MARGIN] += from_left[halo]
                at[CX - MARGIN :] += from_right[halo]
                if t >= PART:
                    turned = at[...].T
                    for h, y in enumerate((t - PART, HALF + PART - 1 - t)):
                        for zg in range(Z // 8):
                            rows = slice(h * Z + zg * 8, h * Z + zg * 8 + 8)
                            flat[pl.ds(zg * 8 * HALF + y, 8, stride=HALF), :] = turned[rows]
                if t in (PART + GROUP - 1, HALF - 1):
                    for copy in copies[:2] if t < HALF - 1 else copies[2:]:
                        copy.start()
            for copy in copies:
                copy.wait()


def spread_rows(part, source, reach, band_z, band_x, *extra):
    partial = (REACHED, CX, CX)
    scratch = [
        pltpu.VMEM((MAIN_SLOTS, GROUP // 2, 2 * CX, 2 * CX), jnp.bfloat16),
        pltpu.VMEM((CLASSES, PART, CX, CX), jnp.float32),
    ]
    if part == 0:
        shapes = [(MARGIN, CX, CX), partial]
        out_specs = [whole(s) for s in shapes]
    else:
        shapes = [(PART, CX, CX), (Z, CY, CX)]
        out_specs = [whole(shapes[0]), pl.BlockSpec(memory_space=pl.ANY)]
        scratch += [
            pltpu.VMEM((HALF + MARGIN, CX, CX), jnp.float32),
            pltpu.VMEM((Z, HALF, CX), jnp.float32),
            pltpu.SemaphoreType.DMA((4,)),
        ]
    steps = PART // GROUP
    return pl.pallas_call(
        functools.partial(rows_kernel, part),
        grid=(steps,),
        out_shape=[jax.ShapeDtypeStruct(s, jnp.float32) for s in shapes],
        in_specs=[
            pl.BlockSpec((GROUP, CX, 2 * CX), lambda i: (i + part * steps, 0, 0)),
            pl.BlockSpec((GROUP, CX, CX), lambda i: (i + part * steps, 0, 0)),
            whole(band_z.shape),
            whole(band_x.shape),
        ]
        + [whole(a.shape) for a in extra],
        out_specs=out_specs,
        scratch_shapes=scratch,
        compiler_params=pltpu.CompilerParams(vmem_limit_bytes=40 * MIB),
        cost_estimate=pl.CostEstimate(flops=8_000_000_000, bytes_accessed=8_000_000, transcendentals=0),
        name="edge_rows" if part == 0 else "middle_rows",
    )(source, reach, band_z, band_x, *extra)


def pack_kernel(halo, from_left, from_right, up_ref, down_ref, line_s):
    upper = lax.broadcasted_iota(jnp.int32, (64, CX), 1) >= Z
    for j in range(MARGIN):
        rows = pl.ds(MARGIN * j, MARGIN)
        line_s[...] = halo[j]
        line_s[:MARGIN] += from_left[rows]
        line_s[CX - MARGIN :] += from_right[rows]
        one, two = line_s[:64], pltpu.roll(line_s[64:], Z, 1)
        up_ref[j] = jnp.where(upper, one, two)
        down_ref[j] = jnp.where(upper, two, one)


def pack(halo, from_left, from_right):
    return pl.pallas_call(
        pack_kernel,
        out_shape=[jax.ShapeDtypeStruct((MARGIN, 64, CX), jnp.float32)] * 2,
        scratch_shapes=[pltpu.VMEM((CX, CX), jnp.float32)],
        compiler_params=pltpu.CompilerParams(vmem_limit_bytes=8 * MIB),
        name="pack_halo",
    )(halo, from_left, from_right)


def merge_kernel(edge, from_low, from_high, _, out, out_s, sem):
    step = pl.program_id(0)
    upper = lax.broadcasted_iota(jnp.int32, (64, CX), 1) >= Z

    def copies(i):
        return [
            pltpu.make_async_copy(out_s.at[i, h], out.at[:, pl.ds(y, GROUP)], sem.at[i, h])
            for h, y in enumerate((i * GROUP, CY - GROUP - i * GROUP))
        ]

    for i in range(PART // GROUP):

        @pl.when(step == i)
        def _():
            for k in range(GROUP):
                value = edge[k]
                if i * GROUP + k < MARGIN:
                    j = MARGIN - 1 - i * GROUP - k
                    low, high = from_low[j], from_high[j]
                    value = value + jnp.concatenate(
                        [pltpu.roll(jnp.where(upper, low, high), Z, 1), jnp.where(upper, high, low)], axis=0
                    )
                turned = value.T
                for h, y in enumerate((k, GROUP - 1 - k)):
                    flat = out_s.at[i, h].reshape(Z * GROUP, CX)
                    for zg in range(Z // 8):
                        rows = slice(h * Z + zg * 8, h * Z + zg * 8 + 8)
                        flat[pl.ds(zg * 8 * GROUP + y, 8, stride=GROUP), :] = turned[rows]
            for copy in copies(i):
                copy.start()

    @pl.when(step == PART // GROUP - 1)
    def _():
        for i in range(PART // GROUP):
            for copy in copies(i):
                copy.wait()


def merge(edge, from_low, from_high, out):
    return pl.pallas_call(
        merge_kernel,
        grid=(PART // GROUP,),
        out_shape=jax.ShapeDtypeStruct((Z, CY, CX), jnp.float32),
        in_specs=[
            pl.BlockSpec((GROUP, CX, CX), lambda i: (i, 0, 0)),
            whole(from_low.shape),
            whole(from_high.shape),
            pl.BlockSpec(memory_space=pl.ANY),
        ],
        out_specs=pl.BlockSpec(memory_space=pl.ANY),
        scratch_shapes=[
            pltpu.VMEM((PART // GROUP, 2, Z, GROUP, CX), jnp.float32),
            pltpu.SemaphoreType.DMA((PART // GROUP, 2)),
        ],
        input_output_aliases={3: 0},
        compiler_params=pltpu.CompilerParams(vmem_limit_bytes=8 * MIB),
        name="merge_rows",
    )(edge, from_low, from_high, out)


def shifted(value, axis, by):
    length = lax.axis_size(axis)
    return lax.ppermute(value, axis, [(i, i + by) for i in range(length) if 0 <= i + by < length])


def per_device(filtered, upstream, radius_map, brick_class, sharpness, threshold):
    band_z, band_x, band_rim = band_tables()
    in_hbm = lambda a: pltpu.with_memory_space_constraint(a, pltpu.HBM)
    fields = [in_hbm(a) for a in (filtered, upstream, radius_map)]
    source, reach, left, right = rim(
        (brick_class, sharpness, threshold), fields, in_hbm(band_z), in_hbm(band_rim)
    )
    from_left = shifted(right, "gx", 1)
    from_right = shifted(left, "gx", -1)
    halo, partial = spread_rows(0, source, reach, band_z, band_x)
    up, down = pack(halo, from_left, from_right)
    from_low = shifted(up, "gy", 1)
    from_high = shifted(down, "gy", -1)
    edge, out = spread_rows(1, source, reach, band_z, band_x, partial, from_left, from_right)
    return merge(edge, from_low, from_high, out)


def solution(mesh):
    return jax.shard_map(
        per_device,
        mesh=mesh,
        in_specs=(
            P(None, "gy", "gx"),
            P(None, "gy", "gx"),
            P(None, "gy", "gx"),
            P("gx", "gy"),
            P(),
            P(),
        ),
        out_specs=P(None, "gy", "gx"),
        check_vma=False,
    )
```

```python
import functools

import jax
import jax.numpy as jnp
import numpy as np
from jax import lax
from jax.experimental import pallas as pl
from jax.experimental.pallas import tpu as pltpu
from jax.sharding import PartitionSpec as P

RMAX = 12
MARGIN = RMAX - 1
CLASSES = RMAX - 1
Z, CY, CX = 64, 64, 128
HALF = CY // 2
GROUP = 8
PART = HALF // 2
REACHED = PART + MARGIN
RIM = 16
RIM_AHEAD = 4
MAIN_AHEAD = 2
MAIN_SLOTS = 4
HALO_ROWS = 480
MIB = 1024 * 1024


def tent(radius, distance):
    return np.maximum(0, radius - np.abs(distance)).astype(np.float32)


def band_tables():
    z, x = np.arange(Z), np.arange(CX)
    outside = np.full(RIM - MARGIN, 8 * CX)
    rim_from = np.concatenate([np.arange(RIM), np.arange(CX - RIM, CX)])
    rim_to = np.concatenate([np.arange(-MARGIN, 0), outside, np.arange(CX, CX + MARGIN), outside])
    rows_z, rows_x, rows_rim = [], [], []
    for radius in range(2, RMAX + 1):
        rows_z.append(np.kron(np.eye(2, dtype=np.float32), tent(radius, z[:, None] - z[None, :])))
        rows_x.append(tent(radius, x[:, None] - x[None, :]))
        rim = tent(radius, rim_to[:, None] - rim_from[None, :])
        rows_rim.append(np.kron(np.eye(4, dtype=np.float32), rim))
    return [jnp.asarray(np.stack(rows).astype(jnp.bfloat16)) for rows in (rows_z, rows_x, rows_rim)]


def split(value):
    high = value.astype(jnp.bfloat16)
    low = (value - high.astype(jnp.float32)).astype(jnp.bfloat16)
    return high, low


def span(reach, edge):
    short = jnp.maximum(0.0, reach - edge)
    return reach * reach - 0.5 * (short * short + short)


def whole(shape):
    return pl.BlockSpec(shape, lambda i: (0,) * len(shape))


def along_z(c, high_low, reach, band_z):
    radius = jnp.bfloat16(c + 2)
    none = jnp.zeros((), jnp.bfloat16)
    pieces = []
    for pair, level in zip(high_low, reach):
        same = level == radius
        pieces.append(jnp.concatenate([jnp.where(same, piece, none) for piece in pair], axis=1))
    both = jnp.concatenate([band_z[c], band_z[c]], axis=0)
    return split(jnp.dot(jnp.concatenate(pieces, axis=0), both, preferred_element_type=jnp.float32))


def spread_y(load, times, total, keep):
    for t in times:
        grown = load(RMAX, t)
        suffix = grown
        for d in range(MARGIN, -1, -1):
            if d < MARGIN:
                if d + 1 >= 2:
                    suffix = suffix + load(d + 1, t)
                grown = grown + suffix
            for target in {t + d, t - d}:
                total[target] = total[target] + grown if target in total else grown
        keep(t - MARGIN, total.pop(t - MARGIN))
    for target in sorted(total):
        keep(target, total[target])


def rim_kernel(
    class_ref, sharp_ref, thresh_ref, fil0, fil1, ups0, ups1, rad0, rad1, band_z, band_rim,
    source_ref, reach_ref, near_ref, next_ref, pair_a, pair_b, level_a, level_b, grown_s, smooth_s, ext_s,
):
    fil, ups, rad = (
        [ref.reshape(Z * GROUP, CX) for ref in pair] for pair in ((fil0, fil1), (ups0, ups1), (rad0, rad1))
    )
    step = pl.program_id(0)
    col, row = lax.axis_index("gx"), lax.axis_index("gy")
    last_col, last_row = lax.axis_size("gx") - 1, lax.axis_size("gy") - 1
    beta, eta = sharp_ref[0], thresh_ref[0]
    one = jnp.ones((8, CX), jnp.float32)
    scale = (beta * one) / (jnp.tanh(beta * eta * one) + jnp.tanh(beta * (1.0 - eta) * one))
    cap = class_ref[0, 0]
    lane = lax.broadcasted_iota(jnp.int32, (8, CX), 1)
    sub = lax.broadcasted_iota(jnp.int32, (8, CX), 0)
    far = jnp.full((8, CX), 4096, jnp.int32)
    edge_x = jnp.minimum(jnp.where(col == 0, lane, far), jnp.where(col == last_col, CX - 1 - lane, far))
    edge_x = (edge_x + 1).astype(jnp.float32)

    def one_row(k, pair_s, level_s):
        sides = []
        for half in (0, 1):
            y = k if half == 0 else GROUP - 1 - k
            at_edge = row == (0 if half == 0 else last_row)
            edge_y = (jnp.where(at_edge, step * GROUP + k, 4096) + 1).astype(jnp.float32)
            for zg in range(Z // 8):
                at = (pl.ds(zg * 8 * GROUP + y, 8, stride=GROUP), slice(None))
                reach = jnp.minimum(rad[half][at], cap).astype(jnp.float32)
                bend = jnp.tanh(beta * (fil[half][at] - eta))
                slope = ups[half][at] * scale * (1.0 - bend * bend)
                weight = span(reach, edge_x) * span(reach, edge_y)
                if zg in (0, 1, 6, 7):
                    z_in = zg * 8 + sub
                    edge_z = (jnp.minimum(z_in, Z - 1 - z_in) + 1).astype(jnp.float32)
                    weight = weight * span(reach, edge_z)
                else:
                    weight = weight * (reach * reach)
                sides.append((slope / weight, reach))
        high, low = split(jnp.concatenate([a for a, _ in sides], axis=0).T)
        level = jnp.concatenate([b for _, b in sides], axis=0).T.astype(jnp.bfloat16)
        source_ref[k, :, :CX] = high
        source_ref[k, :, CX:] = low
        reach_ref[k] = level
        for n, rows in enumerate((slice(0, RIM), slice(CX - RIM, CX))):
            pair_s[k, n, :, :CX] = high[rows]
            pair_s[k, n, :, CX:] = low[rows]
            level_s[k, n] = level[rows]

    def rim_z(c, pair_s, level_s):
        for k in range(0, GROUP, 4):
            both = [(n, side) for n in range(k, k + 4) for side in (0, 1)]
            pairs = [(pair_s[n, side, :, :CX], pair_s[n, side, :, CX:]) for n, side in both]
            high, low = along_z(c, pairs, [level_s[n, side] for n, side in both], band_z)
            lanes = slice(k // 4 * CX, k // 4 * CX + CX)
            grown_s[c, :CX, lanes] = high
            grown_s[c, CX:, lanes] = low

    def rim_x(c):
        both = jnp.concatenate([band_rim[c], band_rim[c]], axis=1)
        moved = jnp.dot(both, grown_s[c], preferred_element_type=jnp.float32)
        for k in range(GROUP):
            lanes = slice(k // 4 * CX, k // 4 * CX + CX)
            rows = slice(k % 4 * 2 * RIM, k % 4 * 2 * RIM + 2 * RIM)
            smooth_s[c, (step - 1) * GROUP + k] = moved[rows, lanes]

    def classes(pair_s, level_s, beside):
        for c in range(RIM_AHEAD):
            rim_z(c, pair_s, level_s)
        for c in range(CLASSES):
            if c + RIM_AHEAD < CLASSES:
                rim_z(c + RIM_AHEAD, pair_s, level_s)
            beside(c)
            rim_x(c)

    def beside(pair_s, level_s):
        def go(c):
            if c < GROUP:
                one_row(c, pair_s, level_s)

        return go

    groups = HALF // GROUP

    @pl.when(step == 0)
    def _():
        @pl.loop(0, GROUP)
        def _(k):
            one_row(k, pair_a, level_a)

    @pl.when((step % 2 == 1) & (step < groups))
    def _():
        classes(pair_a, level_a, beside(pair_b, level_b))

    @pl.when((step % 2 == 0) & (step > 0) & (step < groups))
    def _():
        classes(pair_b, level_b, beside(pair_a, level_a))

    @pl.when(step == groups)
    def _():
        classes(pair_b, level_b, lambda c: None)

        def tile(k, _):
            rows = pl.ds(pl.multiple_of(k * 8, 8), 8)

            def keep(t, value):
                ext_s[t + MARGIN, rows] = value

            spread_y(lambda radius, t: smooth_s[radius - 2, t, rows], range(HALF), {}, keep)
            return 0

        lax.fori_loop(0, 2 * RIM // 8, tile, 0)
        for t in range(-MARGIN, HALF):
            full = ext_s[t + MARGIN]
            if t >= HALF - MARGIN:
                full = full + pltpu.roll(ext_s[2 * HALF - 1 - t + MARGIN], Z, 1)
            left, right = full[:RIM], full[RIM:]
            rows = pl.ds(MARGIN * (t + MARGIN), MARGIN)
            near_ref[rows] = jnp.where(col % 2 == 0, right, left)[:MARGIN]
            next_ref[rows] = jnp.where(col % 2 == 0, left, right)[:MARGIN]
        for ref in (near_ref, next_ref):
            spare = HALO_ROWS - MARGIN * (HALF + MARGIN)
            ref[pl.ds(HALO_ROWS - spare, spare)] = jnp.zeros((spare, CX), jnp.float32)


def rim(scalars, fields, band_z, band_rim):
    groups = HALF // GROUP
    now = lambda i: jnp.minimum(i, groups - 1)
    block = [
        pl.BlockSpec((Z, GROUP, CX), lambda i: (0, now(i), 0)),
        pl.BlockSpec((Z, GROUP, CX), lambda i: (0, 2 * groups - 1 - now(i), 0)),
    ]
    halo = (HALO_ROWS, CX)
    return pl.pallas_call(
        rim_kernel,
        grid=(groups + 1,),
        out_shape=[
            jax.ShapeDtypeStruct((HALF, CX, 2 * CX), jnp.bfloat16),
            jax.ShapeDtypeStruct((HALF, CX, CX), jnp.bfloat16),
            jax.ShapeDtypeStruct(halo, jnp.float32),
            jax.ShapeDtypeStruct(halo, jnp.float32),
        ],
        in_specs=[pl.BlockSpec(memory_space=pltpu.SMEM)] * 3
        + block * 3
        + [whole(band_z.shape), whole(band_rim.shape)],
        out_specs=[
            pl.BlockSpec((GROUP, CX, 2 * CX), lambda i: (now(i), 0, 0)),
            pl.BlockSpec((GROUP, CX, CX), lambda i: (now(i), 0, 0)),
            whole(halo),
            whole(halo),
        ],
        scratch_shapes=[
            pltpu.VMEM((GROUP, 2, RIM, 2 * CX), jnp.bfloat16),
            pltpu.VMEM((GROUP, 2, RIM, 2 * CX), jnp.bfloat16),
            pltpu.VMEM((GROUP, 2, RIM, CX), jnp.bfloat16),
            pltpu.VMEM((GROUP, 2, RIM, CX), jnp.bfloat16),
            pltpu.VMEM((CLASSES, 2 * CX, 2 * CX), jnp.bfloat16),
            pltpu.VMEM((CLASSES, HALF, 2 * RIM, CX), jnp.float32),
            pltpu.VMEM((HALF + 2 * MARGIN, 2 * RIM, CX), jnp.float32),
        ],
        compiler_params=pltpu.CompilerParams(vmem_limit_bytes=24 * MIB),
        cost_estimate=pl.CostEstimate(flops=4_000_000_000, bytes_accessed=11_000_000, transcendentals=524288),
        name="source_and_rim",
    )(*scalars, *[a for a in fields for _ in (0, 1)], band_z, band_rim)


def sides(axis, near, after):
    even = lax.axis_index(axis) % 2 == 0
    return jnp.where(even, after, near), jnp.where(even, near, after)


def rows_kernel(part, *refs):
    source_ref, reach_ref, band_z, band_x = refs[:4]
    if part == 0:
        halo_ref, part_ref = refs[4:6]
        grown_s, smooth_s = refs[6:]
    else:
        part_ref, x_near, x_next, edge_ref, out_ref = refs[4:9]
        grown_s, smooth_s, ext_s, out_s, sem = refs[9:]
    step = pl.program_id(0)
    start = part * PART

    def main_z(c):
        for k in range(0, GROUP, 2):
            pairs = [(source_ref[n, :, :CX], source_ref[n, :, CX:]) for n in (k, k + 1)]
            high, low = along_z(c, pairs, [reach_ref[n] for n in (k, k + 1)], band_z)
            for n in (0, 1):
                here = slice(n * CX, n * CX + CX)
                grown_s[c % MAIN_SLOTS, k // 2, :CX, here] = high[here]
                grown_s[c % MAIN_SLOTS, k // 2, CX:, here] = low[here]

    def main_x(c, group):
        both = jnp.concatenate([band_x[c], band_x[c]], axis=1)
        for k in range(GROUP // 2):
            moved = jnp.dot(both, grown_s[c % MAIN_SLOTS, k], preferred_element_type=jnp.float32)
            smooth_s[c, group * GROUP + 2 * k] = moved[:, :CX]
            smooth_s[c, group * GROUP + 2 * k + 1] = moved[:, CX:]

    def classes(group, beside):
        for c in range(MAIN_AHEAD):
            main_z(c)
        for c in range(CLASSES):
            if c + MAIN_AHEAD < CLASSES:
                main_z(c + MAIN_AHEAD)
            beside(c)
            main_x(c, group)

    def tile(group, rows):
        first = start + group * GROUP

        def place(t):
            if part == 1:
                return ext_s, t
            return (halo_ref, t + MARGIN) if t < 0 else (part_ref, t)

        def keep(t, value):
            ref, at = place(t)
            ref[at, rows] = value

        total = {}
        for t in range(first - MARGIN, first + MARGIN):
            if group > 0:
                ref, at = place(t)
                total[t] = ref[at, rows]
            elif part == 1 and t < REACHED:
                total[t] = part_ref[t, rows]
        load = lambda radius, t: smooth_s[radius - 2, t - start, rows]
        spread_y(load, range(first, first + GROUP), total, keep)

    tiles = CX // 8

    def tiles_beside(c):
        for k in range(c * tiles // CLASSES, (c + 1) * tiles // CLASSES):
            tile(0, slice(k * 8, k * 8 + 8))

    @pl.when(step == 0)
    def _():
        classes(0, lambda c: None)

    @pl.when(step == 1)
    def _():
        classes(1, tiles_beside)

        @pl.loop(0, tiles)
        def _(k):
            tile(1, pl.ds(pl.multiple_of(k * 8, 8), 8))

        if part == 1:
            flat = out_s.reshape(Z * HALF, CX)
            copies = [
                pltpu.make_async_copy(
                    out_s.at[:, pl.ds(y, GROUP)], out_ref.at[:, pl.ds(PART + y, GROUP)], sem.at[n]
                )
                for n, y in enumerate((0, HALF - GROUP, GROUP, HALF - 2 * GROUP))
            ]
            for t in [*range(PART, HALF), *range(PART)]:
                at = edge_ref.at[t] if t < PART else ext_s.at[t]
                if t < PART:
                    at[...] = part_ref[t] if t < start - MARGIN else ext_s[t]
                elif t >= HALF - MARGIN:
                    at[...] += pltpu.roll(ext_s[2 * HALF - 1 - t], Z, 1)
                halo = pl.ds(MARGIN * (t + MARGIN), MARGIN)
                from_left, from_right = sides("gx", x_near[halo], x_next[halo])
                at[:MARGIN] += from_left
                at[CX - MARGIN :] += from_right
                if t >= PART:
                    turned = at[...].T
                    for h, y in enumerate((t - PART, HALF + PART - 1 - t)):
                        for zg in range(Z // 8):
                            rows = slice(h * Z + zg * 8, h * Z + zg * 8 + 8)
                            flat[pl.ds(zg * 8 * HALF + y, 8, stride=HALF), :] = turned[rows]
                if t in (PART + GROUP - 1, HALF - 1):
                    for copy in copies[:2] if t < HALF - 1 else copies[2:]:
                        copy.start()
            for copy in copies:
                copy.wait()


def spread_rows(part, source, reach, band_z, band_x, *extra):
    partial = (REACHED, CX, CX)
    scratch = [
        pltpu.VMEM((MAIN_SLOTS, GROUP // 2, 2 * CX, 2 * CX), jnp.bfloat16),
        pltpu.VMEM((CLASSES, PART, CX, CX), jnp.float32),
    ]
    if part == 0:
        shapes = [(MARGIN, CX, CX), partial]
        out_specs = [whole(s) for s in shapes]
    else:
        shapes = [(PART, CX, CX), (Z, CY, CX)]
        out_specs = [whole(shapes[0]), pl.BlockSpec(memory_space=pl.ANY)]
        scratch += [
            pltpu.VMEM((HALF + MARGIN, CX, CX), jnp.float32),
            pltpu.VMEM((Z, HALF, CX), jnp.float32),
            pltpu.SemaphoreType.DMA((4,)),
        ]
    steps = PART // GROUP
    return pl.pallas_call(
        functools.partial(rows_kernel, part),
        grid=(steps,),
        out_shape=[jax.ShapeDtypeStruct(s, jnp.float32) for s in shapes],
        in_specs=[
            pl.BlockSpec((GROUP, CX, 2 * CX), lambda i: (i + part * steps, 0, 0)),
            pl.BlockSpec((GROUP, CX, CX), lambda i: (i + part * steps, 0, 0)),
            whole(band_z.shape),
            whole(band_x.shape),
        ]
        + [whole(a.shape) for a in extra],
        out_specs=out_specs,
        scratch_shapes=scratch,
        compiler_params=pltpu.CompilerParams(vmem_limit_bytes=40 * MIB),
        cost_estimate=pl.CostEstimate(flops=8_000_000_000, bytes_accessed=8_000_000, transcendentals=0),
        name="edge_rows" if part == 0 else "middle_rows",
    )(source, reach, band_z, band_x, *extra)


def pack_kernel(halo, x_near, x_next, near_ref, next_ref, line_s):
    upper = lax.broadcasted_iota(jnp.int32, (64, CX), 1) >= Z
    for j in range(MARGIN):
        rows = pl.ds(MARGIN * j, MARGIN)
        line_s[...] = halo[j]
        from_left, from_right = sides("gx", x_near[rows], x_next[rows])
        line_s[:MARGIN] += from_left
        line_s[CX - MARGIN :] += from_right
        one, two = line_s[:64], pltpu.roll(line_s[64:], Z, 1)
        next_ref[j], near_ref[j] = sides("gy", jnp.where(upper, one, two), jnp.where(upper, two, one))


def pack(halo, x_near, x_next):
    return pl.pallas_call(
        pack_kernel,
        out_shape=[jax.ShapeDtypeStruct((MARGIN, 64, CX), jnp.float32)] * 2,
        scratch_shapes=[pltpu.VMEM((CX, CX), jnp.float32)],
        compiler_params=pltpu.CompilerParams(vmem_limit_bytes=8 * MIB),
        name="pack_halo",
    )(halo, x_near, x_next)


def merge_kernel(edge, y_near, y_next, _, out, out_s, sem):
    step = pl.program_id(0)
    upper = lax.broadcasted_iota(jnp.int32, (64, CX), 1) >= Z

    def copies(i):
        return [
            pltpu.make_async_copy(out_s.at[i, h], out.at[:, pl.ds(y, GROUP)], sem.at[i, h])
            for h, y in enumerate((i * GROUP, CY - GROUP - i * GROUP))
        ]

    for i in range(PART // GROUP):

        @pl.when(step == i)
        def _():
            for k in range(GROUP):
                value = edge[k]
                if i * GROUP + k < MARGIN:
                    j = MARGIN - 1 - i * GROUP - k
                    low, high = sides("gy", y_near[j], y_next[j])
                    value = value + jnp.concatenate(
                        [pltpu.roll(jnp.where(upper, low, high), Z, 1), jnp.where(upper, high, low)], axis=0
                    )
                turned = value.T
                for h, y in enumerate((k, GROUP - 1 - k)):
                    flat = out_s.at[i, h].reshape(Z * GROUP, CX)
                    for zg in range(Z // 8):
                        rows = slice(h * Z + zg * 8, h * Z + zg * 8 + 8)
                        flat[pl.ds(zg * 8 * GROUP + y, 8, stride=GROUP), :] = turned[rows]
            for copy in copies(i):
                copy.start()

    @pl.when(step == PART // GROUP - 1)
    def _():
        for i in range(PART // GROUP):
            for copy in copies(i):
                copy.wait()


def merge(edge, y_near, y_next, out):
    return pl.pallas_call(
        merge_kernel,
        grid=(PART // GROUP,),
        out_shape=jax.ShapeDtypeStruct((Z, CY, CX), jnp.float32),
        in_specs=[
            pl.BlockSpec((GROUP, CX, CX), lambda i: (i, 0, 0)),
            whole(y_near.shape),
            whole(y_next.shape),
            pl.BlockSpec(memory_space=pl.ANY),
        ],
        out_specs=pl.BlockSpec(memory_space=pl.ANY),
        scratch_shapes=[
            pltpu.VMEM((PART // GROUP, 2, Z, GROUP, CX), jnp.float32),
            pltpu.SemaphoreType.DMA((PART // GROUP, 2)),
        ],
        input_output_aliases={3: 0},
        compiler_params=pltpu.CompilerParams(vmem_limit_bytes=8 * MIB),
        name="merge_rows",
    )(edge, y_near, y_next, out)


def swapped(value, axis, first):
    pairs = [(i, i + 1) for i in range(first, lax.axis_size(axis) - 1, 2)]
    return lax.ppermute(value, axis, pairs + [(b, a) for a, b in pairs])


def per_device(filtered, upstream, radius_map, brick_class, sharpness, threshold):
    band_z, band_x, band_rim = band_tables()
    in_hbm = lambda a: pltpu.with_memory_space_constraint(a, pltpu.HBM)
    fields = [in_hbm(a) for a in (filtered, upstream, radius_map)]
    source, reach, x_near, x_next = rim(
        (brick_class, sharpness, threshold), fields, in_hbm(band_z), in_hbm(band_rim)
    )
    x_next = swapped(x_next, "gx", 1)
    x_near = swapped(x_near, "gx", 0)
    halo, partial = spread_rows(0, source, reach, band_z, band_x)
    y_near, y_next = pack(halo, x_near, x_next)
    y_next = swapped(y_next, "gy", 1)
    y_near = swapped(y_near, "gy", 0)
    edge, out = spread_rows(1, source, reach, band_z, band_x, partial, x_near, x_next)
    return merge(edge, y_near, y_next, out)


def solution(mesh):
    return jax.shard_map(
        per_device,
        mesh=mesh,
        in_specs=(
            P(None, "gy", "gx"),
            P(None, "gy", "gx"),
            P(None, "gy", "gx"),
            P("gx", "gy"),
            P(),
            P(),
        ),
        out_specs=P(None, "gy", "gx"),
        check_vma=False,
    )
```

```python
import functools

import jax
import jax.numpy as jnp
import numpy as np
from jax import lax
from jax.experimental import pallas as pl
from jax.experimental.pallas import tpu as pltpu
from jax.sharding import PartitionSpec as P

RMAX = 12
MARGIN = RMAX - 1
CLASSES = RMAX - 1
Z, CY, CX = 64, 64, 128
HALF = CY // 2
GROUP = 8
PART = HALF // 2
REACHED = PART + MARGIN
RIM = 16
RIM_AHEAD = 11
MAIN_AHEAD = 2
MAIN_SLOTS = 4
HALO_ROWS = 480
MIB = 1024 * 1024


def tent(radius, distance):
    return np.maximum(0, radius - np.abs(distance)).astype(np.float32)


def band_tables():
    z, x = np.arange(Z), np.arange(CX)
    outside = np.full(RIM - MARGIN, 8 * CX)
    rim_from = np.concatenate([np.arange(RIM), np.arange(CX - RIM, CX)])
    rim_to = np.concatenate([np.arange(-MARGIN, 0), outside, np.arange(CX, CX + MARGIN), outside])
    rows_z, rows_x, rows_rim = [], [], []
    for radius in range(2, RMAX + 1):
        rows_z.append(np.kron(np.eye(2, dtype=np.float32), tent(radius, z[:, None] - z[None, :])))
        rows_x.append(tent(radius, x[:, None] - x[None, :]))
        rim = tent(radius, rim_to[:, None] - rim_from[None, :])
        rows_rim.append(np.kron(np.eye(4, dtype=np.float32), rim))
    return [jnp.asarray(np.stack(rows).astype(jnp.bfloat16)) for rows in (rows_z, rows_x, rows_rim)]


def split(value):
    high = value.astype(jnp.bfloat16)
    low = (value - high.astype(jnp.float32)).astype(jnp.bfloat16)
    return high, low


def span(reach, edge):
    short = jnp.maximum(0.0, reach - edge)
    return reach * reach - 0.5 * (short * short + short)


def whole(shape):
    return pl.BlockSpec(shape, lambda i: (0,) * len(shape))


def along_z(c, high_low, reach, band_z):
    radius = jnp.bfloat16(c + 2)
    none = jnp.zeros((), jnp.bfloat16)
    pieces = []
    for pair, level in zip(high_low, reach):
        same = level == radius
        pieces.append(jnp.concatenate([jnp.where(same, piece, none) for piece in pair], axis=1))
    both = jnp.concatenate([band_z[c], band_z[c]], axis=0)
    return split(jnp.dot(jnp.concatenate(pieces, axis=0), both, preferred_element_type=jnp.float32))


def spread_y(load, times, total, keep):
    for t in times:
        grown = load(RMAX, t)
        suffix = grown
        for d in range(MARGIN, -1, -1):
            if d < MARGIN:
                if d + 1 >= 2:
                    suffix = suffix + load(d + 1, t)
                grown = grown + suffix
            for target in {t + d, t - d}:
                total[target] = total[target] + grown if target in total else grown
        keep(t - MARGIN, total.pop(t - MARGIN))
    for target in sorted(total):
        keep(target, total[target])


def rim_kernel(
    class_ref, sharp_ref, thresh_ref, fil0, fil1, ups0, ups1, rad0, rad1, band_z, band_rim,
    source_ref, reach_ref, near_ref, next_ref, pair_a, pair_b, level_a, level_b, grown_s, smooth_s, ext_s,
):
    fil, ups, rad = (
        [ref.reshape(Z * GROUP, CX) for ref in pair] for pair in ((fil0, fil1), (ups0, ups1), (rad0, rad1))
    )
    step = pl.program_id(0)
    col, row = lax.axis_index("gx"), lax.axis_index("gy")
    last_col, last_row = lax.axis_size("gx") - 1, lax.axis_size("gy") - 1
    beta, eta = sharp_ref[0], thresh_ref[0]
    one = jnp.ones((8, CX), jnp.float32)
    scale = (beta * one) / (jnp.tanh(beta * eta * one) + jnp.tanh(beta * (1.0 - eta) * one))
    cap = class_ref[0, 0]
    lane = lax.broadcasted_iota(jnp.int32, (8, CX), 1)
    sub = lax.broadcasted_iota(jnp.int32, (8, CX), 0)
    far = jnp.full((8, CX), 4096, jnp.int32)
    edge_x = jnp.minimum(jnp.where(col == 0, lane, far), jnp.where(col == last_col, CX - 1 - lane, far))
    edge_x = (edge_x + 1).astype(jnp.float32)

    def one_row(k, pair_s, level_s):
        sides = []
        for half in (0, 1):
            y = k if half == 0 else GROUP - 1 - k
            at_edge = row == (0 if half == 0 else last_row)
            edge_y = (jnp.where(at_edge, step * GROUP + k, 4096) + 1).astype(jnp.float32)
            for zg in range(Z // 8):
                at = (pl.ds(zg * 8 * GROUP + y, 8, stride=GROUP), slice(None))
                reach = jnp.minimum(rad[half][at], cap).astype(jnp.float32)
                bend = jnp.tanh(beta * (fil[half][at] - eta))
                slope = ups[half][at] * scale * (1.0 - bend * bend)
                weight = span(reach, edge_x) * span(reach, edge_y)
                if zg in (0, 1, 6, 7):
                    z_in = zg * 8 + sub
                    edge_z = (jnp.minimum(z_in, Z - 1 - z_in) + 1).astype(jnp.float32)
                    weight = weight * span(reach, edge_z)
                else:
                    weight = weight * (reach * reach)
                sides.append((slope / weight, reach))
        high, low = split(jnp.concatenate([a for a, _ in sides], axis=0).T)
        level = jnp.concatenate([b for _, b in sides], axis=0).T.astype(jnp.bfloat16)
        source_ref[k, :, :CX] = high
        source_ref[k, :, CX:] = low
        reach_ref[k] = level
        for n, rows in enumerate((slice(0, RIM), slice(CX - RIM, CX))):
            pair_s[k, n, :, :CX] = high[rows]
            pair_s[k, n, :, CX:] = low[rows]
            level_s[k, n] = level[rows]

    def rim_z(c, pair_s, level_s):
        for k in range(0, GROUP, 4):
            both = [(n, side) for n in range(k, k + 4) for side in (0, 1)]
            pairs = [(pair_s[n, side, :, :CX], pair_s[n, side, :, CX:]) for n, side in both]
            high, low = along_z(c, pairs, [level_s[n, side] for n, side in both], band_z)
            lanes = slice(k // 4 * CX, k // 4 * CX + CX)
            grown_s[c, :CX, lanes] = high
            grown_s[c, CX:, lanes] = low

    def rim_x(c):
        both = jnp.concatenate([band_rim[c], band_rim[c]], axis=1)
        moved = jnp.dot(both, grown_s[c], preferred_element_type=jnp.float32)
        for k in range(GROUP):
            lanes = slice(k // 4 * CX, k // 4 * CX + CX)
            rows = slice(k % 4 * 2 * RIM, k % 4 * 2 * RIM + 2 * RIM)
            smooth_s[c, (step - 1) * GROUP + k] = moved[rows, lanes]

    def classes(pair_s, level_s, beside):
        for c in range(RIM_AHEAD):
            rim_z(c, pair_s, level_s)
        for c in range(CLASSES):
            if c + RIM_AHEAD < CLASSES:
                rim_z(c + RIM_AHEAD, pair_s, level_s)
            beside(c)
            rim_x(c)

    def beside(pair_s, level_s):
        def go(c):
            if c < GROUP:
                one_row(c, pair_s, level_s)

        return go

    groups = HALF // GROUP

    @pl.when(step == 0)
    def _():
        @pl.loop(0, GROUP)
        def _(k):
            one_row(k, pair_a, level_a)

    @pl.when((step % 2 == 1) & (step < groups))
    def _():
        classes(pair_a, level_a, beside(pair_b, level_b))

    @pl.when((step % 2 == 0) & (step > 0) & (step < groups))
    def _():
        classes(pair_b, level_b, beside(pair_a, level_a))

    @pl.when(step == groups)
    def _():
        classes(pair_b, level_b, lambda c: None)

        def tile(k, _):
            rows = pl.ds(pl.multiple_of(k * 8, 8), 8)

            def keep(t, value):
                ext_s[t + MARGIN, rows] = value

            spread_y(lambda radius, t: smooth_s[radius - 2, t, rows], range(HALF), {}, keep)
            return 0

        lax.fori_loop(0, 2 * RIM // 8, tile, 0)
        for t in range(-MARGIN, HALF):
            full = ext_s[t + MARGIN]
            if t >= HALF - MARGIN:
                full = full + pltpu.roll(ext_s[2 * HALF - 1 - t + MARGIN], Z, 1)
            left, right = full[:RIM], full[RIM:]
            rows = pl.ds(MARGIN * (t + MARGIN), MARGIN)
            near_ref[rows] = jnp.where(col % 2 == 0, right, left)[:MARGIN]
            next_ref[rows] = jnp.where(col % 2 == 0, left, right)[:MARGIN]
        for ref in (near_ref, next_ref):
            spare = HALO_ROWS - MARGIN * (HALF + MARGIN)
            ref[pl.ds(HALO_ROWS - spare, spare)] = jnp.zeros((spare, CX), jnp.float32)


def rim(scalars, fields, band_z, band_rim):
    groups = HALF // GROUP
    now = lambda i: jnp.minimum(i, groups - 1)
    block = [
        pl.BlockSpec((Z, GROUP, CX), lambda i: (0, now(i), 0)),
        pl.BlockSpec((Z, GROUP, CX), lambda i: (0, 2 * groups - 1 - now(i), 0)),
    ]
    halo = (HALO_ROWS, CX)
    return pl.pallas_call(
        rim_kernel,
        grid=(groups + 1,),
        out_shape=[
            jax.ShapeDtypeStruct((HALF, CX, 2 * CX), jnp.bfloat16),
            jax.ShapeDtypeStruct((HALF, CX, CX), jnp.bfloat16),
            jax.ShapeDtypeStruct(halo, jnp.float32),
            jax.ShapeDtypeStruct(halo, jnp.float32),
        ],
        in_specs=[pl.BlockSpec(memory_space=pltpu.SMEM)] * 3
        + block * 3
        + [whole(band_z.shape), whole(band_rim.shape)],
        out_specs=[
            pl.BlockSpec((GROUP, CX, 2 * CX), lambda i: (now(i), 0, 0)),
            pl.BlockSpec((GROUP, CX, CX), lambda i: (now(i), 0, 0)),
            whole(halo),
            whole(halo),
        ],
        scratch_shapes=[
            pltpu.VMEM((GROUP, 2, RIM, 2 * CX), jnp.bfloat16),
            pltpu.VMEM((GROUP, 2, RIM, 2 * CX), jnp.bfloat16),
            pltpu.VMEM((GROUP, 2, RIM, CX), jnp.bfloat16),
            pltpu.VMEM((GROUP, 2, RIM, CX), jnp.bfloat16),
            pltpu.VMEM((CLASSES, 2 * CX, 2 * CX), jnp.bfloat16),
            pltpu.VMEM((CLASSES, HALF, 2 * RIM, CX), jnp.float32),
            pltpu.VMEM((HALF + 2 * MARGIN, 2 * RIM, CX), jnp.float32),
        ],
        compiler_params=pltpu.CompilerParams(vmem_limit_bytes=24 * MIB),
        cost_estimate=pl.CostEstimate(flops=4_000_000_000, bytes_accessed=11_000_000, transcendentals=524288),
        name="source_and_rim",
    )(*scalars, *[a for a in fields for _ in (0, 1)], band_z, band_rim)


def sides(axis, near, after):
    even = lax.axis_index(axis) % 2 == 0
    return jnp.where(even, after, near), jnp.where(even, near, after)


def rows_kernel(part, *refs):
    source_ref, reach_ref, band_z, band_x = refs[:4]
    if part == 0:
        halo_ref, part_ref = refs[4:6]
        grown_s, smooth_s = refs[6:]
    else:
        part_ref, x_near, x_next, edge_ref, out_ref = refs[4:9]
        grown_s, smooth_s, ext_s, out_s, sem = refs[9:]
    step = pl.program_id(0)
    start = part * PART

    def main_z(c):
        for k in range(0, GROUP, 2):
            pairs = [(source_ref[n, :, :CX], source_ref[n, :, CX:]) for n in (k, k + 1)]
            high, low = along_z(c, pairs, [reach_ref[n] for n in (k, k + 1)], band_z)
            for n in (0, 1):
                here = slice(n * CX, n * CX + CX)
                grown_s[c % MAIN_SLOTS, k // 2, :CX, here] = high[here]
                grown_s[c % MAIN_SLOTS, k // 2, CX:, here] = low[here]

    def main_x(c, group):
        both = jnp.concatenate([band_x[c], band_x[c]], axis=1)
        for k in range(GROUP // 2):
            moved = jnp.dot(both, grown_s[c % MAIN_SLOTS, k], preferred_element_type=jnp.float32)
            smooth_s[c, group * GROUP + 2 * k] = moved[:, :CX]
            smooth_s[c, group * GROUP + 2 * k + 1] = moved[:, CX:]

    def classes(group, beside):
        for c in range(MAIN_AHEAD):
            main_z(c)
        for c in range(CLASSES):
            if c + MAIN_AHEAD < CLASSES:
                main_z(c + MAIN_AHEAD)
            beside(c)
            main_x(c, group)

    def tile(group, rows):
        first = start + group * GROUP

        def place(t):
            if part == 1:
                return ext_s, t
            return (halo_ref, t + MARGIN) if t < 0 else (part_ref, t)

        def keep(t, value):
            ref, at = place(t)
            ref[at, rows] = value

        total = {}
        for t in range(first - MARGIN, first + MARGIN):
            if group > 0:
                ref, at = place(t)
                total[t] = ref[at, rows]
            elif part == 1 and t < REACHED:
                total[t] = part_ref[t, rows]
        load = lambda radius, t: smooth_s[radius - 2, t - start, rows]
        spread_y(load, range(first, first + GROUP), total, keep)

    tiles = CX // 8

    def tiles_beside(c):
        for k in range(c * tiles // CLASSES, (c + 1) * tiles // CLASSES):
            tile(0, slice(k * 8, k * 8 + 8))

    @pl.when(step == 0)
    def _():
        classes(0, lambda c: None)

    @pl.when(step == 1)
    def _():
        classes(1, tiles_beside)

        @pl.loop(0, tiles)
        def _(k):
            tile(1, pl.ds(pl.multiple_of(k * 8, 8), 8))

        if part == 1:
            flat = out_s.reshape(Z * HALF, CX)
            copies = [
                pltpu.make_async_copy(
                    out_s.at[:, pl.ds(y, GROUP)], out_ref.at[:, pl.ds(PART + y, GROUP)], sem.at[n]
                )
                for n, y in enumerate((0, HALF - GROUP, GROUP, HALF - 2 * GROUP))
            ]
            for t in [*range(PART, HALF), *range(PART)]:
                at = edge_ref.at[t] if t < PART else ext_s.at[t]
                if t < PART:
                    at[...] = part_ref[t] if t < start - MARGIN else ext_s[t]
                elif t >= HALF - MARGIN:
                    at[...] += pltpu.roll(ext_s[2 * HALF - 1 - t], Z, 1)
                halo = pl.ds(MARGIN * (t + MARGIN), MARGIN)
                from_left, from_right = sides("gx", x_near[halo], x_next[halo])
                at[:MARGIN] += from_left
                at[CX - MARGIN :] += from_right
                if t >= PART:
                    turned = at[...].T
                    for h, y in enumerate((t - PART, HALF + PART - 1 - t)):
                        for zg in range(Z // 8):
                            rows = slice(h * Z + zg * 8, h * Z + zg * 8 + 8)
                            flat[pl.ds(zg * 8 * HALF + y, 8, stride=HALF), :] = turned[rows]
                if t in (PART + GROUP - 1, HALF - 1):
                    for copy in copies[:2] if t < HALF - 1 else copies[2:]:
                        copy.start()
            for copy in copies:
                copy.wait()


def spread_rows(part, source, reach, band_z, band_x, *extra):
    partial = (REACHED, CX, CX)
    scratch = [
        pltpu.VMEM((MAIN_SLOTS, GROUP // 2, 2 * CX, 2 * CX), jnp.bfloat16),
        pltpu.VMEM((CLASSES, PART, CX, CX), jnp.float32),
    ]
    if part == 0:
        shapes = [(MARGIN, CX, CX), partial]
        out_specs = [whole(s) for s in shapes]
    else:
        shapes = [(PART, CX, CX), (Z, CY, CX)]
        out_specs = [whole(shapes[0]), pl.BlockSpec(memory_space=pl.ANY)]
        scratch += [
            pltpu.VMEM((HALF + MARGIN, CX, CX), jnp.float32),
            pltpu.VMEM((Z, HALF, CX), jnp.float32),
            pltpu.SemaphoreType.DMA((4,)),
        ]
    steps = PART // GROUP
    return pl.pallas_call(
        functools.partial(rows_kernel, part),
        grid=(steps,),
        out_shape=[jax.ShapeDtypeStruct(s, jnp.float32) for s in shapes],
        in_specs=[
            pl.BlockSpec((GROUP, CX, 2 * CX), lambda i: (i + part * steps, 0, 0)),
            pl.BlockSpec((GROUP, CX, CX), lambda i: (i + part * steps, 0, 0)),
            whole(band_z.shape),
            whole(band_x.shape),
        ]
        + [whole(a.shape) for a in extra],
        out_specs=out_specs,
        scratch_shapes=scratch,
        compiler_params=pltpu.CompilerParams(vmem_limit_bytes=40 * MIB),
        cost_estimate=pl.CostEstimate(flops=8_000_000_000, bytes_accessed=8_000_000, transcendentals=0),
        name="edge_rows" if part == 0 else "middle_rows",
    )(source, reach, band_z, band_x, *extra)


def pack_kernel(halo, x_near, x_next, near_ref, next_ref, line_s):
    upper = lax.broadcasted_iota(jnp.int32, (64, CX), 1) >= Z
    for j in range(MARGIN):
        rows = pl.ds(MARGIN * j, MARGIN)
        line_s[...] = halo[j]
        from_left, from_right = sides("gx", x_near[rows], x_next[rows])
        line_s[:MARGIN] += from_left
        line_s[CX - MARGIN :] += from_right
        one, two = line_s[:64], pltpu.roll(line_s[64:], Z, 1)
        next_ref[j], near_ref[j] = sides("gy", jnp.where(upper, one, two), jnp.where(upper, two, one))


def pack(halo, x_near, x_next):
    return pl.pallas_call(
        pack_kernel,
        out_shape=[jax.ShapeDtypeStruct((MARGIN, 64, CX), jnp.float32)] * 2,
        scratch_shapes=[pltpu.VMEM((CX, CX), jnp.float32)],
        compiler_params=pltpu.CompilerParams(vmem_limit_bytes=8 * MIB),
        name="pack_halo",
    )(halo, x_near, x_next)


def merge_kernel(edge, y_near, y_next, _, out, out_s, sem):
    step = pl.program_id(0)
    upper = lax.broadcasted_iota(jnp.int32, (64, CX), 1) >= Z

    def copies(i):
        return [
            pltpu.make_async_copy(out_s.at[i, h], out.at[:, pl.ds(y, GROUP)], sem.at[i, h])
            for h, y in enumerate((i * GROUP, CY - GROUP - i * GROUP))
        ]

    for i in range(PART // GROUP):

        @pl.when(step == i)
        def _():
            for k in range(GROUP):
                value = edge[k]
                if i * GROUP + k < MARGIN:
                    j = MARGIN - 1 - i * GROUP - k
                    low, high = sides("gy", y_near[j], y_next[j])
                    value = value + jnp.concatenate(
                        [pltpu.roll(jnp.where(upper, low, high), Z, 1), jnp.where(upper, high, low)], axis=0
                    )
                turned = value.T
                for h, y in enumerate((k, GROUP - 1 - k)):
                    flat = out_s.at[i, h].reshape(Z * GROUP, CX)
                    for zg in range(Z // 8):
                        rows = slice(h * Z + zg * 8, h * Z + zg * 8 + 8)
                        flat[pl.ds(zg * 8 * GROUP + y, 8, stride=GROUP), :] = turned[rows]
            for copy in copies(i):
                copy.start()

    @pl.when(step == PART // GROUP - 1)
    def _():
        for i in range(PART // GROUP):
            for copy in copies(i):
                copy.wait()


def merge(edge, y_near, y_next, out):
    return pl.pallas_call(
        merge_kernel,
        grid=(PART // GROUP,),
        out_shape=jax.ShapeDtypeStruct((Z, CY, CX), jnp.float32),
        in_specs=[
            pl.BlockSpec((GROUP, CX, CX), lambda i: (i, 0, 0)),
            whole(y_near.shape),
            whole(y_next.shape),
            pl.BlockSpec(memory_space=pl.ANY),
        ],
        out_specs=pl.BlockSpec(memory_space=pl.ANY),
        scratch_shapes=[
            pltpu.VMEM((PART // GROUP, 2, Z, GROUP, CX), jnp.float32),
            pltpu.SemaphoreType.DMA((PART // GROUP, 2)),
        ],
        input_output_aliases={3: 0},
        compiler_params=pltpu.CompilerParams(vmem_limit_bytes=8 * MIB),
        name="merge_rows",
    )(edge, y_near, y_next, out)


def swapped(value, axis, first):
    pairs = [(i, i + 1) for i in range(first, lax.axis_size(axis) - 1, 2)]
    return lax.ppermute(value, axis, pairs + [(b, a) for a, b in pairs])


def per_device(filtered, upstream, radius_map, brick_class, sharpness, threshold):
    band_z, band_x, band_rim = band_tables()
    in_hbm = lambda a: pltpu.with_memory_space_constraint(a, pltpu.HBM)
    fields = [in_hbm(a) for a in (filtered, upstream, radius_map)]
    source, reach, x_near, x_next = rim(
        (brick_class, sharpness, threshold), fields, in_hbm(band_z), in_hbm(band_rim)
    )
    x_near = swapped(x_near, "gx", 0)
    x_next = swapped(x_next, "gx", 1)
    halo, partial = spread_rows(0, source, reach, band_z, band_x)
    y_near, y_next = pack(halo, x_near, x_next)
    y_near = swapped(y_near, "gy", 0)
    y_next = swapped(y_next, "gy", 1)
    edge, out = spread_rows(1, source, reach, band_z, band_x, partial, x_near, x_next)
    return merge(edge, y_near, y_next, out)


def solution(mesh):
    return jax.shard_map(
        per_device,
        mesh=mesh,
        in_specs=(
            P(None, "gy", "gx"),
            P(None, "gy", "gx"),
            P(None, "gy", "gx"),
            P("gx", "gy"),
            P(),
            P(),
        ),
        out_specs=P(None, "gy", "gx"),
        check_vma=False,
    )
```
